128 devices in a mesh: row: 8 (over z, core), col: 16 (over y, x).
Axes of the slice: x: 4, y: 4, z: 4, core: 2. Of those that a mesh axis runs over, the one named last changes fastest.
Arguments:
- base: bfloat16 [256, 512, 256], P('row', 'col'), may hold values from -6 to 6
- observations: bfloat16 [65536, 128], P(('row', 'col')), may hold values from -6 to 6
- destination: int32 [65536, 1], P(('row', 'col')), may hold values from 0 to 127; in each aligned block of 512 rows (0 to 511, 512 to 1023, ...) at most 8 rows name the same one
- cell_index: int32 [65536], P(('row', 'col')), may hold values from 0 to 1023
- shard_counts: int32 [128], P(('row', 'col')), may hold values from 1 to 512, 49152 in all
- embed_weight: bfloat16 [128, 256], replicated, may hold values from -0.5 to 0.5
- conv_weights: bfloat16 [3, 9, 256, 256], replicated, may hold values from -0.125 to 0.125
- cotangent: bfloat16 [256, 512, 256], P('row', 'col'), may hold values from -6 to 6
Outputs:
- block_out: bfloat16 [256, 512, 256], P('row', 'col')
- base_grad: float32 [256, 512, 256], P('row', 'col')
- conv_grads: float32 [3, 9, 256, 256], replicated
- embed_grad: float32 [128, 256], replicated
The draws below stay inside these ranges and needn't reach their ends.
Inputs may be any that keep to these rules, and one draw needn't show every extreme that they name: `destination`: among the 512 rows of one ingestion shard, live or not, at most 8 name the same tile. `shard_counts`: rows of a shard at positions from its count on are ignored.
All inputs are finite; a program needn't handle non-finite values.
Results may differ from the reference program's by a relative error of at most 0.017.
Values may be sent and summed in bfloat16 or wider, within the bound.
A program may use at most 128 MiB of HBM per device.

```python
import math
import jax
import jax.numpy as jnp
import numpy as np
from jax import lax

C = 256
OBS = 128
LAYERS = 3
H_DEV = 32
W_DEV = 32
S_DEV = 512
CAP = 8
NH = 256
NW = 512
STATIONS = 65536
N_COL = 16
DEVICES = 128


def place_ends(drawn, stream_key, low, high):
    extent = drawn.shape
    index_at = [jax.random.randint(jax.random.fold_in(stream_key, axis), (), 0, extent[axis]) for axis in range(len(extent))]
    drawn = drawn.at[tuple(index_at)].set(low)
    longest = extent.index(max(extent))
    index_at[longest] = (index_at[longest] + 1) % extent[longest]
    return drawn.at[tuple(index_at)].set(high)


def block_scale(key, dims, split, low, top_value):
    def one(axis_at, parts):
        draws = jax.random.uniform(jax.random.fold_in(jax.random.fold_in(key, 6), axis_at), (parts,), jnp.float32, low / len(split), top_value / len(split))
        return jnp.repeat(jnp.exp(draws), dims[axis_at] // parts).reshape((-1,) + (1,) * (len(dims) - axis_at - 1))

    factor_of = one(*split[0])
    for cut in split[1:]:
        factor_of = factor_of * one(*cut)
    return factor_of


def split_up(number_of, total, reach, skew):
    loads = [(1 << 20) // math.isqrt(grade ** skew) + 1 for grade in range(2, number_of + 1)]
    rest, given = total - reach - (number_of - 1), [1] * (number_of - 1)
    while rest > 0:
        movable = [i for i in range(number_of - 1) if given[i] < reach]
        whole, left = sum([loads[i] for i in movable]), rest
        for i in movable:
            addition = min(reach - given[i], max(1, left * loads[i] // whole), rest)
            given[i] = given[i] + addition
            rest = rest - addition
    return np.array([reach] + given)


def ragged(rng, count, total, reach, lean):
    if count == 2:
        one = jax.random.randint(rng, (), max(1, total - reach), min(reach, total - 1) + 1)
        return jnp.stack([one, total - one])
    lengths = jnp.asarray(split_up(count, total, reach, lean), jnp.int32)
    couples = (count - 1) // 2
    giver, taker = lengths[1:1 + 2 * couples:2], lengths[2:2 + 2 * couples:2]
    margin = jnp.minimum(giver - 1, reach - taker)
    moved = jax.random.randint(jax.random.fold_in(rng, 1), (couples,), 0, 1 << 20) % (margin + 1)
    lengths = lengths.at[1:1 + 2 * couples:2].set(giver - moved).at[2:2 + 2 * couples:2].set(taker + moved)
    return lengths[jax.random.permutation(jax.random.fold_in(rng, 2), count)]


def shared_out(stream_key, own, number, rows, count, top, most, lean):
    order = jax.random.permutation(stream_key, count)
    heavy_load, usual = shares(count, rows * top, most, lean, True), shares(count, rows * top, most, lean, False)
    places = jnp.arange(count)

    def named(tallies, rotation):
        used = int((tallies > 0).sum())
        fixed = max(1, used // 4)
        moved = fixed + (places - fixed + rotation * (used - fixed)) % max(1, count - fixed)
        return jnp.zeros((count,), jnp.int32).at[order[jnp.where(places < fixed, places, moved)]].set(jnp.asarray(tallies, jnp.int32))

    tallies = jnp.where(number % 4 == 0, named(heavy_load, number // 4), named(usual, number - number // 4 - 1))
    mixed = jax.random.permutation(jax.random.fold_in(own, 3), count)
    source_of, sink = mixed[0:count // 2 * 2:2], mixed[1:count // 2 * 2:2]
    room = jnp.minimum(tallies[source_of] - 1, most - tallies[sink]) // 2
    room = jnp.where((source_of == order[0]) | (sink == order[0]) | (tallies[sink] == 0), 0, jnp.maximum(room, 0))
    moved = jax.random.randint(jax.random.fold_in(own, 4), (count // 2,), 0, 1 << 20) % (room + 1)
    tallies = tallies.at[source_of].add(-moved).at[sink].add(moved)
    labels = jnp.searchsorted(jnp.cumsum(tallies), jnp.arange(rows * top), side="right").astype(jnp.int32)
    grid = labels.reshape(top, rows).T
    grid = grid[jax.random.permutation(jax.random.fold_in(own, 1), rows)]
    rotation = jax.random.randint(jax.random.fold_in(own, 2), (rows, 1), 0, top)
    return jnp.take_along_axis(grid, (jnp.arange(top)[None, :] + rotation) % top, axis=1)


def shares(count, total, bound, skew, full):
    portions = [(1 << 20) // math.isqrt(grade ** skew) + 1 for grade in range(1, count + 1)]
    largest = bound if full else min(bound, max(-(-total // count), total * portions[0] // sum(portions)))
    least = 1 if total - largest >= count - 1 else 0
    counts, rest = [largest] + [least] * (count - 1), total - largest - least * (count - 1)
    while rest > 0:
        movable = [i for i in range(1, count) if counts[i] < largest] or [i for i in range(1, count) if counts[i] < bound]
        whole, left = sum([portions[i] for i in movable]), rest
        for i in movable:
            more = min(bound - counts[i], max(1, left * portions[i] // whole), rest)
            counts[i] = counts[i] + more
            rest = rest - more
    return np.array(counts)


def noise(rng, dims, width, most, shards=(), kind=jnp.bfloat16):
    gain = block_scale(rng, dims, shards, -0.22, 0.18) if shards else 1.0
    array = jax.random.normal(rng, dims, jnp.float32) * width * gain
    return jnp.minimum(jnp.maximum(array, -most), most).astype(kind)


def setup_inputs(seed: int = 0) -> dict:
    key_of = jax.random.split(jax.random.key(seed), 9)
    base = noise(key_of[0], (NH, NW, C), 1.0, 6.0, ((0, 8), (1, 16)))
    observations = noise(key_of[1], (STATIONS, OBS), 1.0, 6.0, ((0, 128),))
    destination_keys = jax.random.split(jax.random.fold_in(key_of[2], 1), STATIONS // S_DEV)
    destination_turns = jax.random.permutation(jax.random.fold_in(key_of[2], 3), STATIONS // S_DEV)
    destination = jax.vmap(lambda own, number: shared_out(jax.random.fold_in(key_of[2], 2), own, number, S_DEV, DEVICES, 1, CAP, 2))(destination_keys, destination_turns).reshape((STATIONS, 1))
    cell_index = place_ends(jax.random.randint(key_of[3], (STATIONS,), 0, H_DEV * W_DEV), jax.random.fold_in(key_of[3], 1), 0, (H_DEV * W_DEV) - 1).astype(jnp.int32)
    shard_counts = ragged(key_of[4], DEVICES, 3 * S_DEV * DEVICES // 4, S_DEV, 2).astype(jnp.int32)
    embed_weight = noise(key_of[5], (OBS, C), OBS ** -0.5, 0.5)
    conv_weights = noise(key_of[6], (LAYERS, 9, C, C), (9 * C) ** -0.5, 0.125)
    cotangent = noise(key_of[7], (NH, NW, C), 1.0, 6.0, ((0, 8), (1, 16)))
    return dict(base=base, observations=observations, destination=destination, cell_index=cell_index, shard_counts=shard_counts, embed_weight=embed_weight, conv_weights=conv_weights, cotangent=cotangent)


def unfold(padded, spacing, tile_rows, tile_cols):
    pieces = [padded[i * spacing:i * spacing + tile_rows, j * spacing:j * spacing + tile_cols, :] for i in range(3) for j in range(3)]
    return jnp.concatenate(pieces, axis=-1).reshape(tile_rows * tile_cols, -1)

def reference(base, observations, destination, cell_index, shard_counts, embed_weight, conv_weights, cotangent):
    grid_rows, grid_cols, channels = base.shape
    ncells = grid_rows * grid_cols
    position = jnp.arange(STATIONS, dtype=jnp.int32)
    live = position % S_DEV < shard_counts[position // S_DEV]
    target = destination[:, 0]
    glob_row = target // N_COL * H_DEV + cell_index // W_DEV
    glob_col = target % N_COL * W_DEV + cell_index % W_DEV
    flat_cell = jnp.where(live, glob_row * grid_cols + glob_col, ncells).astype(jnp.int32)
    embedded = jnp.dot(observations, embed_weight, preferred_element_type=jnp.float32).astype(jnp.bfloat16)
    placed = jax.ops.segment_sum(embedded.astype(jnp.float32), flat_cell, num_segments=ncells + 1)[:ncells]
    hidden = (base.astype(jnp.float32) + placed.reshape(grid_rows, grid_cols, channels)).astype(jnp.bfloat16)
    saved = []
    for layer_id in range(LAYERS):
        spacing = 2 ** layer_id
        active = jax.nn.silu(hidden.astype(jnp.float32)).astype(jnp.bfloat16)
        padded = jnp.pad(active, ((spacing, spacing), (spacing, spacing), (0, 0)))
        update = jnp.dot(unfold(padded, spacing, grid_rows, grid_cols), conv_weights[layer_id].reshape(9 * channels, channels), preferred_element_type=jnp.float32)
        saved.append((hidden, padded))
        hidden = (hidden.astype(jnp.float32) + update.reshape(grid_rows, grid_cols, channels)).astype(jnp.bfloat16)
    block_out = hidden
    scale = 1.0 / math.sqrt(ncells)
    grad = cotangent.astype(jnp.float32)
    kernels = [None] * LAYERS
    for layer_id in reversed(range(LAYERS)):
        spacing = 2 ** layer_id
        hidden_in, padded = saved[layer_id]
        grad_low = grad.astype(jnp.bfloat16)
        kernel = lax.dot_general(unfold(padded, spacing, grid_rows, grid_cols), grad_low.reshape(ncells, channels), (((0,), (0,)), ((), ())), preferred_element_type=jnp.float32)
        kernels[layer_id] = kernel.reshape(9, channels, channels) * scale
        flipped = jnp.swapaxes(conv_weights[layer_id][::-1], 1, 2).reshape(9 * channels, channels)
        grad_pad = jnp.pad(grad_low, ((spacing, spacing), (spacing, spacing), (0, 0)))
        back = jnp.dot(unfold(grad_pad, spacing, grid_rows, grid_cols), flipped, preferred_element_type=jnp.float32).reshape(grid_rows, grid_cols, channels)
        hidden_f = hidden_in.astype(jnp.float32)
        sigma = jax.nn.sigmoid(hidden_f)
        grad = grad + back * sigma * (1.0 + hidden_f * (1.0 - sigma))
    grad_low = grad.astype(jnp.bfloat16).reshape(ncells, channels)
    station_grad = jnp.where(live[:, None], grad_low[jnp.minimum(flat_cell, ncells - 1)], jnp.zeros((), jnp.bfloat16))
    embed_grad = lax.dot_general(observations, station_grad, (((0,), (0,)), ((), ())), preferred_element_type=jnp.float32) * scale
    return (block_out, grad, jnp.stack(kernels), embed_grad)
```

```python
import math

import jax
import jax.numpy as jnp
from jax import lax
from jax.experimental import pallas as pl
from jax.experimental.pallas import tpu as pltpu
from jax.sharding import PartitionSpec as P

LAYERS = 3
MESH = pl.DeviceIdType.MESH


class Place:
    def __init__(self):
        row, col = lax.axis_index("row"), lax.axis_index("col")
        self.core = lax.rem(row, 2)
        self.at = {"z": lax.div(row, 2), "y": lax.div(col, 4), "x": lax.rem(col, 4)}

    def device(self, **changed):
        at = {**self.at, "core": self.core, **changed}
        return (at["z"] * 2 + at["core"], at["y"] * 4 + at["x"])

    def other(self, axis, step):
        return lax.rem(self.at[axis] + step, 4)

    def sibling(self):
        return self.device(core=1 - self.core)

    def all_peers(self):
        peers = [self.sibling()]
        for axis in "xyz":
            peers += [self.device(**{axis: self.other(axis, step)}) for step in (1, 2, 3)]
        return peers


ORDERS = (("x", "y", "z"), ("y", "z", "x"), ("z", "x", "y"))


def f32(value):
    return value.astype(jnp.float32)


def low(value):
    return value.astype(jnp.bfloat16)


class KernelSum:
    def __init__(self, place, layer, refs):
        self.place, self.layer, self.refs = place, layer, refs
        self.steps = [
            self.swap, self.scatter_a, self.scatter_b, self.share_c, self.gather_b, self.gather_a,
            self.swap_back, self.end,
        ]

    def remote(self, src, dst, sems, device):
        return pltpu.make_async_remote_copy(
            src_ref=src, dst_ref=dst, send_sem=sems[0], recv_sem=sems[1], device_id=device, device_id_type=MESH
        )

    def sems(self, phase, group, step):
        r = self.refs
        return r["send"].at[self.layer, group, phase, step - 1], r["recv"].at[self.layer, group, phase, step - 1]

    def swap_copy(self, back):
        r, l, core = self.refs, self.layer, self.place.core
        sems = r["swap_send"].at[l, back], r["swap_recv"].at[l, back]
        if back:
            return self.remote(r["out"].at[l, core], r["out"].at[l, core], sems, self.place.sibling())
        return self.remote(r["part"].at[l, 1 - core], r["sib"].at[l], sems, self.place.sibling())

    def copies(self, phase):
        r, l, core = self.refs, self.layer, self.place.core
        result = []
        for group, (a, b, c) in enumerate(ORDERS):
            axis = (a, b, c, b, a)[phase]
            mine = self.place.at[axis]
            for step in (1, 2, 3):
                to = self.place.other(axis, step)
                src, dst = [
                    lambda: (r["a_own"].at[l, group, to], r["a_in"].at[l, group, step - 1]),
                    lambda: (r["b_own"].at[l, group, to], r["b_in"].at[l, group, step - 1]),
                    lambda: (r["c_all"].at[l, group, mine], r["c_all"].at[l, group, mine]),
                    lambda: (r["b_res"].at[l, group, mine], r["b_res"].at[l, group, mine]),
                    lambda: (r["b_res"].at[l, group], r["out"].at[l, core, group, mine]),
                ][phase]()
                result.append(self.remote(src, dst, self.sems(phase, group, step), self.place.device(**{axis: to})))
        return result

    def start(self, phase):
        for copy in self.copies(phase):
            copy.start()

    def wait(self, phase):
        for copy in self.copies(phase):
            copy.wait()

    def swap(self):
        self.swap_copy(0).start()

    def scatter_a(self):
        r, l, core = self.refs, self.layer, self.place.core
        self.swap_copy(0).wait()
        for group in range(3):
            r["a_own"][l, group] = low(f32(r["part"][l, core, group]) + f32(r["sib"][l, group]))
        self.start(0)

    def scatter_b(self):
        r, l = self.refs, self.layer
        self.wait(0)
        for group, (a, b, c) in enumerate(ORDERS):
            total = f32(r["a_own"][l, group, self.place.at[a]])
            for step in range(3):
                total += f32(r["a_in"][l, group, step])
            r["b_own"][l, group] = low(total).reshape(4, 48, 128)
        self.start(1)

    def share_c(self):
        r, l = self.refs, self.layer
        self.wait(1)
        for group, (a, b, c) in enumerate(ORDERS):
            total = f32(r["b_own"][l, group, self.place.at[b]])
            for step in range(3):
                total += f32(r["b_in"][l, group, step])
            r["c_all"][l, group, self.place.at[c]] = low(total)
        self.start(2)

    def gather_b(self):
        r, l = self.refs, self.layer
        self.wait(2)
        for group, (a, b, c) in enumerate(ORDERS):
            total = f32(r["c_all"][l, group, 0])
            for index in (1, 2, 3):
                total += f32(r["c_all"][l, group, index])
            r["b_res"][l, group, self.place.at[b]] = low(total)
        self.start(3)

    def gather_a(self):
        r, l, core = self.refs, self.layer, self.place.core
        self.wait(3)
        self.start(4)
        for group, (a, b, c) in enumerate(ORDERS):
            r["out"][l, core, group, self.place.at[a]] = r["b_res"][l, group]

    def swap_back(self):
        self.wait(4)
        self.swap_copy(1).start()

    def end(self):
        self.swap_copy(1).wait()


class EmbedSum(KernelSum):
    def __init__(self, place, refs):
        self.place, self.refs = place, refs
        self.steps = [self.swap, self.scatter, self.share_y, self.share_x, self.gather, self.swap_back, self.end]

    def swap_copy(self, back):
        r, core = self.refs, self.place.core
        sems = r["e_swap_send"].at[back], r["e_swap_recv"].at[back]
        if back:
            return self.remote(r["e_out"].at[core], r["e_out"].at[core], sems, self.place.sibling())
        return self.remote(r["e_part"].at[1 - core], r["e_sib"], sems, self.place.sibling())

    def copies(self, phase):
        r, core = self.refs, self.place.core
        axis = ("z", "y", "x", "z")[phase]
        mine, result = self.place.at[axis], []
        for step in (1, 2, 3):
            to = self.place.other(axis, step)
            src, dst = [
                lambda: (r["e_own"].at[to], r["e_in"].at[step - 1]),
                lambda: (r["e_y"].at[mine], r["e_y"].at[mine]),
                lambda: (r["e_x"].at[mine], r["e_x"].at[mine]),
                lambda: (r["e_res"], r["e_out"].at[core, mine]),
            ][phase]()
            sems = r["e_send"].at[phase, step - 1], r["e_recv"].at[phase, step - 1]
            result.append(self.remote(src, dst, sems, self.place.device(**{axis: to})))
        return result

    def scatter(self):
        r = self.refs
        self.swap_copy(0).wait()
        r["e_own"][...] = low(f32(r["e_part"][self.place.core]) + f32(r["e_sib"][...]))
        self.start(0)

    def share_y(self):
        r = self.refs
        self.wait(0)
        total = f32(r["e_own"][self.place.at["z"]])
        for step in range(3):
            total += f32(r["e_in"][step])
        r["e_y"][self.place.at["y"]] = low(total)
        self.start(1)

    def share_x(self):
        r = self.refs
        self.wait(1)
        total = f32(r["e_y"][0])
        for index in (1, 2, 3):
            total += f32(r["e_y"][index])
        r["e_x"][self.place.at["x"]] = low(total)
        self.start(2)

    def gather(self):
        r = self.refs
        self.wait(2)
        total = f32(r["e_x"][0])
        for index in (1, 2, 3):
            total += f32(r["e_x"][index])
        r["e_res"][...] = low(total)
        self.start(3)
        r["e_out"][self.place.core, self.place.at["z"]] = low(total)

    def swap_back(self):
        self.wait(3)
        self.swap_copy(1).start()


BF = jnp.bfloat16
SUM_SCRATCH = dict(
    sib=pltpu.VMEM((3, 3, 4, 192, 128), BF),
    a_own=pltpu.VMEM((3, 3, 4, 192, 128), BF),
    a_in=pltpu.VMEM((3, 3, 3, 192, 128), BF),
    b_own=pltpu.VMEM((3, 3, 4, 48, 128), BF),
    b_in=pltpu.VMEM((3, 3, 3, 48, 128), BF),
    c_all=pltpu.VMEM((3, 3, 4, 48, 128), BF),
    b_res=pltpu.VMEM((3, 3, 4, 48, 128), BF),
    e_sib=pltpu.VMEM((4, 32, 128), BF),
    e_own=pltpu.VMEM((4, 32, 128), BF),
    e_in=pltpu.VMEM((3, 32, 128), BF),
    e_y=pltpu.VMEM((4, 32, 128), BF),
    e_x=pltpu.VMEM((4, 32, 128), BF),
    e_res=pltpu.VMEM((32, 128), BF),
    send=pltpu.SemaphoreType.DMA((3, 3, 5, 3)),
    recv=pltpu.SemaphoreType.DMA((3, 3, 5, 3)),
    swap_send=pltpu.SemaphoreType.DMA((3, 2)),
    swap_recv=pltpu.SemaphoreType.DMA((3, 2)),
    e_send=pltpu.SemaphoreType.DMA((4, 3)),
    e_recv=pltpu.SemaphoreType.DMA((4, 3)),
    e_swap_send=pltpu.SemaphoreType.DMA((2,)),
    e_swap_recv=pltpu.SemaphoreType.DMA((2,)),
)


def greet(peers):
    barrier = pltpu.get_barrier_semaphore()
    for peer in peers:
        pl.semaphore_signal(barrier, inc=1, device_id=peer, device_id_type=MESH)
    pl.semaphore_wait(barrier, len(peers))


def sum_kernel(part, e_part, out, e_out, *scratch):
    refs = dict(zip(SUM_SCRATCH, scratch), part=part, e_part=e_part, out=out, e_out=e_out)
    place = Place()
    greet(place.all_peers())
    streams = [KernelSum(place, 2, refs), KernelSum(place, 1, refs), KernelSum(place, 0, refs), EmbedSum(place, refs)]
    for turn in range(max(len(s.steps) for s in streams)):
        for stream in streams:
            if turn < len(stream.steps):
                stream.steps[turn]()


def sum_all(part, e_part):
    vmem = pl.BlockSpec(memory_space=pltpu.VMEM)
    return pl.pallas_call(
        sum_kernel,
        out_shape=[
            jax.ShapeDtypeStruct((3, 2, 3, 4, 4, 48, 128), BF),
            jax.ShapeDtypeStruct((2, 4, 32, 128), BF),
        ],
        in_specs=[vmem, vmem],
        out_specs=[vmem, vmem],
        scratch_shapes=list(SUM_SCRATCH.values()),
        compiler_params=pltpu.CompilerParams(
            collective_id=0, has_side_effects=True, vmem_limit_bytes=48 * 2**20
        ),
    )(part, e_part)


def padded_2(array, sides, width):
    for axis, dim in sides:
        devices, length = (lax.axis_size(axis), array.shape[dim])
        up = [(i, (i + 1) % devices) for i in range(devices - 1)]
        down = [(j, i) for i, j in up]
        last = lax.slice_in_dim(array, length - width, length, axis=dim)
        first = lax.slice_in_dim(array, 0, width, axis=dim)
        before = lax.ppermute(last, axis, up)
        after = lax.ppermute(first, axis, down)
        array = jnp.concatenate([before, array, after], axis=dim)
    return array


def unfold(padded, spacing, tile_rows, tile_cols):
    pieces = [
        padded[i * spacing : i * spacing + tile_rows, j * spacing : j * spacing + tile_cols, :]
        for i in range(3)
        for j in range(3)
    ]
    return jnp.concatenate(pieces, axis=-1).reshape(tile_rows * tile_cols, -1)


def local(
    base, observations, destination, cell_index, shard_counts, embed_weight, conv_weights, cotangent
):
    tile_rows, tile_cols, channels = base.shape
    n_rowdev = lax.axis_size("row")
    n_coldev = lax.axis_size("col")
    devices = n_rowdev * n_coldev
    shard_rows = observations.shape[0]
    slots = max(2, 2 * shard_rows // devices)
    local_cells = tile_rows * tile_cols
    scale = 1.0 / math.sqrt(local_cells * devices)
    target = destination[:, 0]
    position = jnp.arange(shard_rows, dtype=jnp.int32)
    live = position < shard_counts[0]
    marks = (target[:, None] == jnp.arange(devices, dtype=jnp.int32)[None, :]).astype(jnp.int32)
    rank = jnp.sum(jnp.cumsum(marks, axis=0) * marks, axis=1) - 1
    slot_of = target * slots + rank
    outgoing = (
        jnp.zeros((devices * slots, observations.shape[1]), observations.dtype)
        .at[slot_of]
        .set(observations)
    )
    out_cells = (
        jnp.full((devices * slots,), -1, jnp.int32).at[slot_of].set(jnp.where(live, cell_index, -1))
    )
    incoming, in_cells = (
        lax.all_to_all(
            outgoing.reshape(devices, slots, -1),
            ("row", "col"),
            split_axis=0,
            concat_axis=0,
            tiled=True,
        ),
        lax.all_to_all(
            out_cells.reshape(devices, slots),
            ("row", "col"),
            split_axis=0,
            concat_axis=0,
            tiled=True,
        ),
    )
    incoming = incoming.reshape(devices * slots, -1)
    in_cells = in_cells.reshape(devices * slots)
    embedded = jnp.dot(incoming, embed_weight, preferred_element_type=jnp.float32).astype(
        jnp.bfloat16
    )
    picker = (jnp.arange(local_cells, dtype=jnp.int32)[:, None] == in_cells[None, :]).astype(
        jnp.bfloat16
    )
    placed = jnp.dot(picker, embedded, preferred_element_type=jnp.float32)
    hidden = (base.astype(jnp.float32) + placed.reshape(tile_rows, tile_cols, channels)).astype(
        jnp.bfloat16
    )
    saved = []
    for layer_id in range(LAYERS):
        spacing = 2**layer_id
        active = jax.nn.silu(hidden.astype(jnp.float32)).astype(jnp.bfloat16)
        padded = padded_2(active, (("row", 0), ("col", 1)), spacing)
        update = jnp.dot(
            unfold(padded, spacing, tile_rows, tile_cols),
            conv_weights[layer_id].reshape(9 * channels, channels),
            preferred_element_type=jnp.float32,
        )
        saved.append((hidden, padded))
        hidden = (
            hidden.astype(jnp.float32) + update.reshape(tile_rows, tile_cols, channels)
        ).astype(jnp.bfloat16)
    grad = cotangent.astype(jnp.float32)
    kernels = [None] * LAYERS
    for layer_id in reversed(range(LAYERS)):
        spacing = 2**layer_id
        hidden_in, padded = saved[layer_id]
        grad_low = grad.astype(jnp.bfloat16)
        kernel = lax.dot_general(
            unfold(padded, spacing, tile_rows, tile_cols),
            grad_low.reshape(local_cells, channels),
            (((0,), (0,)), ((), ())),
            preferred_element_type=jnp.float32,
        )
        kernels[layer_id] = kernel
        flipped = jnp.swapaxes(conv_weights[layer_id][::-1], 1, 2).reshape(9 * channels, channels)
        grad_pad = padded_2(grad_low, (("row", 0), ("col", 1)), spacing)
        back = jnp.dot(
            unfold(grad_pad, spacing, tile_rows, tile_cols),
            flipped,
            preferred_element_type=jnp.float32,
        ).reshape(tile_rows, tile_cols, channels)
        hidden_f = hidden_in.astype(jnp.float32)
        sigma = jax.nn.sigmoid(hidden_f)
        grad = grad + back * sigma * (1.0 + hidden_f * (1.0 - sigma))
    grad_low = grad.astype(jnp.bfloat16).reshape(local_cells, channels)
    station_grad = lax.dot_general(
        picker, grad_low, (((0,), (0,)), ((), ())), preferred_element_type=jnp.float32
    ).astype(jnp.bfloat16)
    embed_part = lax.dot_general(
        incoming, station_grad, (((0,), (0,)), ((), ())), preferred_element_type=jnp.float32
    )
    part = jnp.stack(kernels).astype(BF).reshape(3, 2304, 2, 128).transpose(0, 2, 1, 3)
    part = part.reshape(3, 2, 3, 4, 192, 128)
    e_part = embed_part.astype(BF).reshape(128, 2, 128).transpose(1, 0, 2).reshape(2, 4, 32, 128)
    total, e_total = sum_all(part, e_part)
    total = total.reshape(3, 2, 2304, 128).transpose(0, 2, 1, 3).reshape(LAYERS, 9, channels, channels)
    conv_grads = total.astype(jnp.float32) * scale
    embed_grad = e_total.reshape(2, 128, 128).transpose(1, 0, 2).reshape(128, 256).astype(jnp.float32) * scale
    return (hidden, grad, conv_grads, embed_grad)


def solution(mesh):
    return jax.shard_map(
        local,
        mesh=mesh,
        in_specs=(
            P("row", "col", None),
            P(("row", "col"), None),
            P(("row", "col"), None),
            P(("row", "col")),
            P(("row", "col")),
            P(),
            P(),
            P("row", "col", None),
        ),
        out_specs=(P("row", "col", None), P("row", "col", None), P(), P()),
        check_vma=False,
    )
```

```python
import math

import jax
import jax.numpy as jnp
from jax import lax
from jax.experimental import pallas as pl
from jax.experimental.pallas import tpu as pltpu
from jax.sharding import PartitionSpec as P

MESH = pl.DeviceIdType.MESH
BF = jnp.bfloat16
F32 = jnp.float32
ORDERS = (("x", "y", "z"), ("y", "z", "x"), ("z", "x", "y"))
EXT = 48
DEVICES = 128


def f32(value):
    return value.astype(F32)


def low(value):
    return value.astype(BF)


class Place:
    def __init__(self):
        self.row, self.col = lax.axis_index("row"), lax.axis_index("col")
        self.index = self.row * 16 + self.col
        self.core = lax.rem(self.row, 2)
        self.at = {"z": lax.div(self.row, 2), "y": lax.div(self.col, 4), "x": lax.rem(self.col, 4)}

    def device(self, **changed):
        at = {**self.at, "core": self.core, **changed}
        return (at["z"] * 2 + at["core"], at["y"] * 4 + at["x"])

    def other(self, axis, step):
        return lax.rem(self.at[axis] + step, 4)

    def sibling(self):
        return self.device(core=1 - self.core)

    def grid_neighbour(self, down, right):
        return (lax.rem(self.row + 8 + down, 8), lax.rem(self.col + 16 + right, 16))

    def by_step(self, step):
        number = lax.rem(self.index + step, DEVICES)
        return number, (lax.div(number, 16), lax.rem(number, 16))


def remote(src, dst, sems, device):
    return pltpu.make_async_remote_copy(
        src_ref=src, dst_ref=dst, send_sem=sems[0], recv_sem=sems[1], device_id=device, device_id_type=MESH
    )


def part_of(index, size):
    return pl.ds(pl.multiple_of(index * size, size), size)


class KernelSum:
    def __init__(self, place, layer, refs):
        self.place, self.layer, self.refs = place, layer, refs
        self.lanes = part_of(place.core, 128)
        self.steps = [
            self.swap, self.scatter_a, self.scatter_b, self.share_c, self.gather_b, self.gather_a,
            self.swap_back, self.end,
        ]

    def swap_copy(self, back):
        r, l, core = self.refs, self.layer, self.place.core
        sems = r.swap_send.at[l, back], r.swap_recv.at[l, back]
        if back:
            mine = r.out.at[l, :, :, :, :, self.lanes]
            return remote(mine, mine, sems, self.place.sibling())
        return remote(r.part.at[l, 1 - core], r.sib.at[l], sems, self.place.sibling())

    def copies(self, phase):
        r, l = self.refs, self.layer
        result = []
        for group, (a, b, c) in enumerate(ORDERS):
            axis = (a, b, c, b, a)[phase]
            mine = self.place.at[axis]
            for step in (1, 2, 3):
                to = self.place.other(axis, step)
                src, dst = [
                    lambda: (r.a_own.at[l, group, part_of(to, 192)], r.a_in.at[l, group, step - 1]),
                    lambda: (r.b_own.at[l, group, to], r.b_in.at[l, group, step - 1]),
                    lambda: (r.c_all.at[l, group, mine], r.c_all.at[l, group, mine]),
                    lambda: (r.b_res.at[l, group, mine], r.b_res.at[l, group, mine]),
                    lambda: (r.b_res.at[l, group], r.out.at[l, group, mine, :, :, self.lanes]),
                ][phase]()
                sems = r.send.at[l, group, phase, step - 1], r.recv.at[l, group, phase, step - 1]
                result.append(remote(src, dst, sems, self.place.device(**{axis: to})))
        return result

    def start(self, phase):
        for copy in self.copies(phase):
            copy.start()

    def wait(self, phase):
        for copy in self.copies(phase):
            copy.wait()

    def swap(self):
        self.swap_copy(0).start()

    def scatter_a(self):
        r, l, core = self.refs, self.layer, self.place.core
        self.swap_copy(0).wait()
        for group in range(3):
            r.a_own[l, group] = low(f32(r.part[l, core, group]) + f32(r.sib[l, group]))
        self.start(0)

    def scatter_b(self):
        r, l = self.refs, self.layer
        self.wait(0)
        for group, (a, b, c) in enumerate(ORDERS):
            total = f32(r.a_own[l, group, part_of(self.place.at[a], 192)])
            for step in range(3):
                total += f32(r.a_in[l, group, step])
            r.b_own[l, group] = low(total).reshape(4, 48, 128)
        self.start(1)

    def share_c(self):
        r, l = self.refs, self.layer
        self.wait(1)
        for group, (a, b, c) in enumerate(ORDERS):
            total = f32(r.b_own[l, group, self.place.at[b]])
            for step in range(3):
                total += f32(r.b_in[l, group, step])
            r.c_all[l, group, self.place.at[c]] = low(total)
        self.start(2)

    def gather_b(self):
        r, l = self.refs, self.layer
        self.wait(2)
        for group, (a, b, c) in enumerate(ORDERS):
            total = f32(r.c_all[l, group, 0])
            for index in (1, 2, 3):
                total += f32(r.c_all[l, group, index])
            r.b_res[l, group, self.place.at[b]] = low(total)
        self.start(3)

    def gather_a(self):
        r, l = self.refs, self.layer
        self.wait(3)
        self.start(4)
        for group, (a, b, c) in enumerate(ORDERS):
            r.out[l, group, self.place.at[a], :, :, self.lanes] = r.b_res[l, group]

    def swap_back(self):
        self.wait(4)
        self.swap_copy(1).start()

    def end(self):
        self.swap_copy(1).wait()


class EmbedSum(KernelSum):
    def __init__(self, place, refs):
        self.place, self.refs = place, refs
        self.lanes = part_of(place.core, 128)
        self.steps = [self.swap, self.scatter, self.share_y, self.share_x, self.gather, self.swap_back, self.end]

    def swap_copy(self, back):
        r, core = self.refs, self.place.core
        sems = r.e_swap_send.at[back], r.e_swap_recv.at[back]
        if back:
            mine = r.e_out.at[:, :, self.lanes]
            return remote(mine, mine, sems, self.place.sibling())
        return remote(r.e_part.at[1 - core], r.e_sib, sems, self.place.sibling())

    def copies(self, phase):
        r = self.refs
        axis = ("z", "y", "x", "z")[phase]
        mine, result = self.place.at[axis], []
        for step in (1, 2, 3):
            to = self.place.other(axis, step)
            src, dst = [
                lambda: (r.e_own.at[to], r.e_in.at[step - 1]),
                lambda: (r.e_y.at[mine], r.e_y.at[mine]),
                lambda: (r.e_x.at[mine], r.e_x.at[mine]),
                lambda: (r.e_res, r.e_out.at[mine, :, self.lanes]),
            ][phase]()
            sems = r.e_send.at[phase, step - 1], r.e_recv.at[phase, step - 1]
            result.append(remote(src, dst, sems, self.place.device(**{axis: to})))
        return result

    def scatter(self):
        r = self.refs
        self.swap_copy(0).wait()
        r.e_own[...] = low(f32(r.e_part[self.place.core]) + f32(r.e_sib[...]))
        self.start(0)

    def share_y(self):
        r = self.refs
        self.wait(0)
        total = f32(r.e_own[self.place.at["z"]])
        for step in range(3):
            total += f32(r.e_in[step])
        r.e_y[self.place.at["y"]] = low(total)
        self.start(1)

    def share_x(self):
        r = self.refs
        self.wait(1)
        total = f32(r.e_y[0])
        for index in (1, 2, 3):
            total += f32(r.e_y[index])
        r.e_x[self.place.at["x"]] = low(total)
        self.start(2)

    def gather(self):
        r = self.refs
        self.wait(2)
        total = f32(r.e_x[0])
        for index in (1, 2, 3):
            total += f32(r.e_x[index])
        r.e_res[...] = low(total)
        self.start(3)
        r.e_out[self.place.at["z"], :, self.lanes] = low(total)

    def swap_back(self):
        self.wait(3)
        self.swap_copy(1).start()


def sigmoid(x):
    return 0.5 * jnp.tanh(0.5 * x) + 0.5


def silu_slope(hidden):
    sig = sigmoid(hidden)
    return sig * (1.0 + hidden * (1.0 - sig))


SIDES = ((0, -1), (0, 1), (-1, -1), (-1, 1), (1, -1), (1, 1))


class Halo:
    def __init__(self, place, refs, which, ext):
        self.place, self.refs, self.which, self.ext = place, refs, which, ext

    def copies(self):
        r, ext, result = self.refs, self.ext, []
        up, down = ext.at[8:16, 0:32], ext.at[32:40, 0:32]
        pairs = [((-1, 0), up, ext.at[40:48, 0:32]), ((1, 0), down, ext.at[0:8, 0:32])]
        for number, side in enumerate(SIDES):
            rows = part_of(number * 1, 256) if number < 2 else pl.ds(512 + (number - 2) * 64, 64)
            pairs.append((side, r.strip_out.at[self.which, rows], r.strip_in.at[self.which, rows]))
        for number, (side, src, dst) in enumerate(pairs):
            sems = r.halo_send.at[self.which, number], r.halo_recv.at[self.which, number]
            result.append(remote(src, dst, sems, self.place.grid_neighbour(*side)))
        return result

    def rows_of(self, number):
        return slice(number * 256, number * 256 + 256) if number < 2 else slice(512 + (number - 2) * 64, 576 + (number - 2) * 64)

    def start(self):
        r, ext = self.refs, self.ext
        for number, (down, right) in enumerate(SIDES):
            rows = {0: slice(8, 40), -1: slice(8, 16), 1: slice(32, 40)}[down]
            half = f32(ext[rows, 0:16] if right < 0 else ext[rows, 16:32])
            strip = half[:, 0:8] if right < 0 else half[:, 8:16]
            r.strip_out[self.which, self.rows_of(number)] = low(strip.reshape(-1, 256))
        for copy in self.copies():
            copy.start()

    def end(self):
        r, ext = self.refs, self.ext
        for copy in self.copies():
            copy.wait()
        for down, rows in ((0, slice(8, 40)), (1, slice(0, 8)), (-1, slice(40, 48))):
            strips = []
            for right in (-1, 1):
                strip = f32(r.strip_in[self.which, self.rows_of(SIDES.index((down, right)))])
                strips.append(strip.reshape(-1, 8, 256))
            ext[rows, 32:48] = low(jnp.concatenate(strips, axis=1))


class Stations:
    def __init__(self, place, refs):
        self.place, self.refs = place, refs

    def route(self):
        r = self.refs
        target = r.meta[:, 0:1]
        cell = r.meta[:, 1:2]
        lane = lax.broadcasted_iota(jnp.int32, (512, DEVICES), 1)
        marks = jnp.where(target == lane, 1.0, 0.0)
        earlier = lax.broadcasted_iota(jnp.int32, (512, 512), 0) > lax.broadcasted_iota(jnp.int32, (512, 512), 1)
        before = jnp.dot(low(jnp.where(earlier, 1.0, 0.0)), low(marks), preferred_element_type=F32)
        rank = jnp.sum(before * marks, axis=1, keepdims=True)
        slot = f32(target) * 8.0 + rank
        picks = low(jnp.where(slot == f32(lax.broadcasted_iota(jnp.int32, (512, 1024), 1)), 1.0, 0.0))
        where = jnp.where(lane < 64, cell >> 5, cell & 31)
        info = low(f32(jnp.where(cell >= 0, where + 1, 0)))
        across = (((0,), (0,)), ((), ()))
        rows = lax.dot_general(picks, r.obs[...], across, preferred_element_type=F32).reshape(DEVICES, 8, 128)
        cells = lax.dot_general(picks, info, across, preferred_element_type=F32).reshape(DEVICES, 8, 128)
        r.st_out[...] = low(jnp.concatenate([rows, cells], axis=1))

    def send(self):
        r, place = self.refs, self.place

        def one(step, carry):
            number, device = place.by_step(step)
            remote(r.st_out.at[number], r.st_in.at[place.index], (r.st_send, r.st_recv), device).start()
            return carry

        lax.fori_loop(1, DEVICES, one, 0)
        r.st_in[place.index] = r.st_out[place.index]

    def receive(self):
        r = self.refs
        all_in = r.st_in.at[pl.ds(0, DEVICES - 1)]
        remote(all_in, all_in, (r.st_send, r.st_recv), self.place.by_step(1)[1]).wait()
        blocks = f32(r.st_in[...])
        r.rows[...] = low(blocks[:, 0:8].reshape(1024, 128))
        info = blocks[:, 8:16].reshape(1024, 128)
        r.cell_col[...] = info[:, 0:1] * 32.0 + info[:, 64:65] - 33.0
        turned = info.T
        cell_row = turned[0:1, :] * 32.0 + turned[64:65, :] - 33.0
        embedded = low(jnp.dot(r.rows[...], r.embed[...], preferred_element_type=F32))
        for part in range(4):
            cells = f32(lax.broadcasted_iota(jnp.int32, (256, 1024), 0) + part * 256)
            picks = low(jnp.where(cells == cell_row, 1.0, 0.0))
            placed = jnp.dot(picks, embedded, preferred_element_type=F32).reshape(8, 32, 256)
            own = slice(part * 8, part * 8 + 8)
            r.hid[0, part * 8 + 8 : part * 8 + 16, 0:32] = low(f32(r.base[own]) + placed)

    def gradient(self, grad_low):
        r = self.refs
        for part in range(2):
            rows = slice(part * 512, part * 512 + 512)
            cells = f32(lax.broadcasted_iota(jnp.int32, (512, 1024), 1))
            picks = low(jnp.where(cells == r.cell_col[rows], 1.0, 0.0))
            picked = low(jnp.dot(picks, grad_low, preferred_element_type=F32))
            total = lax.dot_general(r.rows[rows], picked, (((0,), (0,)), ((), ())), preferred_element_type=F32)
            yield total


def greet():
    place, barrier = Place(), pltpu.get_barrier_semaphore()

    def one(step, carry):
        pl.semaphore_signal(barrier, inc=1, device_id=place.by_step(step)[1], device_id_type=MESH)
        return carry

    lax.fori_loop(1, DEVICES, one, 0)
    return lambda: pl.semaphore_wait(barrier, DEVICES - 1)


class Convs:
    def __init__(self, place, refs):
        self.place, self.refs = place, refs

    def inside(self, first, rows):
        row = lax.broadcasted_iota(jnp.int32, (rows, EXT, 256), 0) + (first - 8 + self.place.row * 32)
        col = lax.broadcasted_iota(jnp.int32, (rows, EXT, 256), 1)
        col = jnp.where(col < 40, col, col - EXT) + self.place.col * 32
        return (row >= 0) & (row < 256) & (col >= 0) & (col < 512)

    def spread(self, value_of, out, spacing, sign, rows):
        first, last, size = rows

        def one(step, carry):
            row = first + step * size
            value = jnp.where(self.inside(row, size), value_of(row, size), 0.0)
            out[1, pl.ds(row, size)] = low(value)
            out[1 - sign, pl.ds(row, size)] = low(jnp.roll(value, spacing, axis=1))
            out[1 + sign, pl.ds(row, size)] = low(jnp.roll(value, -spacing, axis=1))
            return carry

        lax.fori_loop(0, (last - first) // size, one, 0)

    def activate(self, layer, rows):
        hid = self.refs.hid.at[layer]

        def value(row, size):
            x = f32(hid[pl.ds(row, size)])
            return x * sigmoid(x)

        self.spread(value, self.refs.act.at[layer], 2**layer, 1, rows)

    def taps(self, source, weights, row, size, width, spacing, sign, turned):
        total = None
        for i in range(3):
            for j in range(3):
                cells = source[j, pl.ds(row + sign * (i - 1) * spacing, size), 0:width].reshape(size * width, 256)
                contract = (((1,), (1 if turned else 0,)), ((), ()))
                term = lax.dot_general(cells, weights[3 * i + j], contract, preferred_element_type=F32)
                total = term if total is None else total + term
        return total.reshape(size, width, 256)

    def forward(self, layer, rows, width=EXT):
        r, (first, last, size) = self.refs, rows

        def one(step, carry):
            row = first + step * size
            update = self.taps(r.act.at[layer], r.weights.at[layer], row, size, width, 2**layer, 1, False)
            result = low(f32(r.hid[layer, pl.ds(row, size), 0:width]) + update)
            if layer == 2:
                r.block_out[pl.ds(row - 8, size)] = result
            else:
                r.hid[layer + 1, pl.ds(row, size)] = result
            return carry

        lax.fori_loop(0, (last - first) // size, one, 0)

    def kernel(self, layer):
        r, spacing = self.refs, 2**layer
        grad = r.grad_low[1, 8:40, 0:32].reshape(1024, 256)

        def one(j, carry):
            for i in range(3):
                row = 8 + (i - 1) * spacing
                cells = r.act[layer, j, row : row + 32, 0:32].reshape(1024, 256)
                total = lax.dot_general(cells, grad, (((0,), (0,)), ((), ())), preferred_element_type=F32)
                for half in range(2):
                    r.part[layer, half, i, part_of(j, 256)] = low(total[:, half * 128 : half * 128 + 128])
            return carry

        lax.fori_loop(0, 3, one, 0)

    def back(self, layer, rows, width=EXT):
        r, (first, last, size) = self.refs, rows

        def one(step, carry):
            row = first + step * size
            update = self.taps(r.grad_low, r.weights.at[layer], row, size, width, 2**layer, -1, True)
            before = f32(r.cot[pl.ds(row, size)]) if layer == 2 else r.grad[pl.ds(row, size), 0:width]
            result = before + update * silu_slope(f32(r.hid[layer, pl.ds(row, size), 0:width]))
            if layer == 0:
                r.base_grad[pl.ds(row - 8, size)] = result
            else:
                r.grad[pl.ds(row, size)] = result
            return carry

        lax.fori_loop(0, (last - first) // size, one, 0)

    def spread_grad(self, layer, rows):
        r = self.refs

        def value(row, size):
            return f32(r.cot[pl.ds(row, size)]) if layer == 2 else r.grad[pl.ds(row, size)]

        self.spread(value, r.grad_low, 2**layer, -1, rows)


class Refs:
    def __init__(self, names, refs):
        self.__dict__.update(zip(names, refs))


def whole_kernel(names, *refs):
    r = Refs(names, refs)
    place = Place()
    finish_greeting = greet()
    fetch = pltpu.make_async_copy(r.weights_hbm, r.weights, r.fetch)
    fetch.start()
    stations, convs = Stations(place, r), Convs(place, r)
    stations.route()
    r.cot[8:40, 0:32] = r.cotangent[...]
    halo_cot, halo_hid = Halo(place, r, 0, r.cot), Halo(place, r, 1, r.hid.at[0])
    finish_greeting()
    stations.send()
    halo_cot.start()
    stations.receive()
    halo_hid.start()
    halo_cot.end()
    convs.spread_grad(2, (0, 48, 4))
    fetch.wait()
    halo_hid.end()
    convs.activate(0, (0, 48, 4))
    convs.forward(0, (2, 46, 11))
    convs.activate(1, (2, 46, 4))
    convs.forward(1, (4, 44, 10))
    convs.activate(2, (4, 44, 4))
    convs.forward(2, (8, 40, 16), 32)

    sums = {layer: KernelSum(place, layer, r).steps for layer in range(3)}
    sums["e"] = EmbedSum(place, r).steps

    def step(*which):
        for name in which:
            sums[name].pop(0)()

    convs.kernel(2)
    step(2)
    convs.back(2, (4, 24, 10))
    step(2)
    convs.back(2, (24, 44, 10))
    step(2)
    convs.spread_grad(1, (4, 44, 4))
    convs.kernel(1)
    step(2, 1)
    convs.back(1, (6, 24, 9))
    step(2, 1)
    convs.back(1, (24, 42, 9))
    step(2, 1)
    convs.spread_grad(0, (6, 42, 4))
    convs.kernel(0)
    step(2, 1, 0)
    convs.back(0, (8, 40, 16), 32)
    step(2, 1, 0)
    grad_low = low(r.base_grad[...].reshape(1024, 256))
    first, second = stations.gradient(grad_low)
    total = first + second
    for half in range(2):
        r.e_part[half] = low(total[:, half * 128 : half * 128 + 128]).reshape(4, 32, 128)
    step("e")
    while any(sums.values()):
        step(*[name for name in (1, 0, "e") if sums[name]])


SUM_SCRATCH = dict(
    part=pltpu.VMEM((3, 2, 3, 768, 128), BF),
    sib=pltpu.VMEM((3, 3, 768, 128), BF),
    a_own=pltpu.VMEM((3, 3, 768, 128), BF),
    a_in=pltpu.VMEM((3, 3, 3, 192, 128), BF),
    b_own=pltpu.VMEM((3, 3, 4, 48, 128), BF),
    b_in=pltpu.VMEM((3, 3, 3, 48, 128), BF),
    c_all=pltpu.VMEM((3, 3, 4, 48, 128), BF),
    b_res=pltpu.VMEM((3, 3, 4, 48, 128), BF),
    e_part=pltpu.VMEM((2, 4, 32, 128), BF),
    e_sib=pltpu.VMEM((4, 32, 128), BF),
    e_own=pltpu.VMEM((4, 32, 128), BF),
    e_in=pltpu.VMEM((3, 32, 128), BF),
    e_y=pltpu.VMEM((4, 32, 128), BF),
    e_x=pltpu.VMEM((4, 32, 128), BF),
    e_res=pltpu.VMEM((32, 128), BF),
    send=pltpu.SemaphoreType.DMA((3, 3, 5, 3)),
    recv=pltpu.SemaphoreType.DMA((3, 3, 5, 3)),
    swap_send=pltpu.SemaphoreType.DMA((3, 2)),
    swap_recv=pltpu.SemaphoreType.DMA((3, 2)),
    e_send=pltpu.SemaphoreType.DMA((4, 3)),
    e_recv=pltpu.SemaphoreType.DMA((4, 3)),
    e_swap_send=pltpu.SemaphoreType.DMA((2,)),
    e_swap_recv=pltpu.SemaphoreType.DMA((2,)),
)
SCRATCH = dict(
    SUM_SCRATCH,
    weights=pltpu.VMEM((3, 9, 256, 256), BF),
    fetch=pltpu.SemaphoreType.DMA,
    st_out=pltpu.VMEM((DEVICES, 16, 128), BF),
    st_in=pltpu.VMEM((DEVICES, 16, 128), BF),
    st_send=pltpu.SemaphoreType.DMA,
    st_recv=pltpu.SemaphoreType.DMA,
    rows=pltpu.VMEM((1024, 128), BF),
    cell_col=pltpu.VMEM((1024, 1), F32),
    cot=pltpu.VMEM((EXT, EXT, 256), BF),
    hid=pltpu.VMEM((3, EXT, EXT, 256), BF),
    act=pltpu.VMEM((3, 3, EXT, EXT, 256), BF),
    grad_low=pltpu.VMEM((3, EXT, EXT, 256), BF),
    grad=pltpu.VMEM((EXT, EXT, 256), F32),
    strip_out=pltpu.VMEM((2, 768, 256), BF),
    strip_in=pltpu.VMEM((2, 768, 256), BF),
    halo_send=pltpu.SemaphoreType.DMA((2, 8)),
    halo_recv=pltpu.SemaphoreType.DMA((2, 8)),
)
INPUTS = ("base", "obs", "meta", "embed", "weights_hbm", "cotangent")
OUTPUTS = ("block_out", "base_grad", "out", "e_out")


def local(
    base, observations, destination, cell_index, shard_counts, embed_weight, conv_weights, cotangent
):
    live = jnp.arange(512, dtype=jnp.int32) < shard_counts[0]
    meta = jnp.concatenate([destination, jnp.where(live, cell_index, -1)[:, None]], axis=1)
    vmem, anywhere = pl.BlockSpec(memory_space=pltpu.VMEM), pl.BlockSpec(memory_space=pl.ANY)
    names = INPUTS + OUTPUTS + tuple(SCRATCH)
    block_out, base_grad, total, e_total = pl.pallas_call(
        lambda *refs: whole_kernel(names, *refs),
        out_shape=[
            jax.ShapeDtypeStruct((32, 32, 256), BF),
            jax.ShapeDtypeStruct((32, 32, 256), F32),
            jax.ShapeDtypeStruct((3, 3, 4, 4, 48, 256), BF),
            jax.ShapeDtypeStruct((4, 32, 256), BF),
        ],
        in_specs=[vmem, vmem, vmem, vmem, anywhere, vmem],
        out_specs=[vmem, vmem, vmem, vmem],
        scratch_shapes=list(SCRATCH.values()),
        compiler_params=pltpu.CompilerParams(
            collective_id=0, has_side_effects=True, vmem_limit_bytes=60 * 2**20
        ),
        name="station_block",
    )(base, observations, meta, embed_weight, conv_weights, cotangent)
    scale = 1.0 / math.sqrt(131072)
    conv_grads = total.reshape(3, 9, 256, 256).astype(F32) * scale
    embed_grad = e_total.reshape(128, 256).astype(F32) * scale
    return (block_out, base_grad, conv_grads, embed_grad)


def solution(mesh):
    return jax.shard_map(
        local,
        mesh=mesh,
        in_specs=(
            P("row", "col", None),
            P(("row", "col"), None),
            P(("row", "col"), None),
            P(("row", "col")),
            P(("row", "col")),
            P(),
            P(),
            P("row", "col", None),
        ),
        out_specs=(P("row", "col", None), P("row", "col", None), P(), P()),
        check_vma=False,
    )
```

```python
import math

import jax
import jax.numpy as jnp
from jax import lax
from jax.experimental import pallas as pl
from jax.experimental.pallas import tpu as pltpu
from jax.sharding import PartitionSpec as P

MESH = pl.DeviceIdType.MESH
BF = jnp.bfloat16
F32 = jnp.float32
ORDERS = (("x", "y", "z"), ("y", "z", "x"), ("z", "x", "y"))
EXT = 48
DEVICES = 128


def f32(value):
    return value.astype(F32)


def low(value):
    return value.astype(BF)


class Place:
    def __init__(self):
        self.row, self.col = lax.axis_index("row"), lax.axis_index("col")
        self.index = self.row * 16 + self.col
        self.core = lax.rem(self.row, 2)
        self.at = {"z": lax.div(self.row, 2), "y": lax.div(self.col, 4), "x": lax.rem(self.col, 4)}

    def device(self, **changed):
        at = {**self.at, "core": self.core, **changed}
        return (at["z"] * 2 + at["core"], at["y"] * 4 + at["x"])

    def other(self, axis, step):
        return lax.rem(self.at[axis] + step, 4)

    def sibling(self):
        return self.device(core=1 - self.core)

    def grid_neighbour(self, down, right):
        return (lax.rem(self.row + 8 + down, 8), lax.rem(self.col + 16 + right, 16))

    def by_step(self, step):
        number = lax.rem(self.index + step, DEVICES)
        return number, (lax.div(number, 16), lax.rem(number, 16))


def remote(src, dst, sems, device):
    return pltpu.make_async_remote_copy(
        src_ref=src, dst_ref=dst, send_sem=sems[0], recv_sem=sems[1], device_id=device, device_id_type=MESH
    )


def part_of(index, size):
    return pl.ds(pl.multiple_of(index * size, size), size)


class KernelSum:
    def __init__(self, place, layer, refs):
        self.place, self.layer, self.refs = place, layer, refs
        self.lanes = part_of(place.core, 128)
        self.steps = [
            self.swap, self.scatter_a, self.scatter_b, self.share_c, self.gather_b, self.gather_a,
            self.swap_back, self.end,
        ]

    def swap_copy(self, back):
        r, l, core = self.refs, self.layer, self.place.core
        sems = r.swap_send.at[l, back], r.swap_recv.at[l, back]
        if back:
            mine = r.out.at[l, :, :, :, :, self.lanes]
            return remote(mine, mine, sems, self.place.sibling())
        return remote(r.part.at[l, 1 - core], r.sib.at[l], sems, self.place.sibling())

    def copies(self, phase):
        r, l = self.refs, self.layer
        result = []
        for group, (a, b, c) in enumerate(ORDERS):
            axis = (a, b, c, b, a)[phase]
            mine = self.place.at[axis]
            for step in (1, 2, 3):
                to = self.place.other(axis, step)
                src, dst = [
                    lambda: (r.a_own.at[l, group, part_of(to, 192)], r.a_in.at[l, group, step - 1]),
                    lambda: (r.b_own.at[l, group, to], r.b_in.at[l, group, step - 1]),
                    lambda: (r.c_all.at[l, group, mine], r.c_all.at[l, group, mine]),
                    lambda: (r.b_res.at[l, group, mine], r.b_res.at[l, group, mine]),
                    lambda: (r.b_res.at[l, group], r.out.at[l, group, mine, :, :, self.lanes]),
                ][phase]()
                sems = r.send.at[l, group, phase, step - 1], r.recv.at[l, group, phase, step - 1]
                result.append(remote(src, dst, sems, self.place.device(**{axis: to})))
        return result

    def start(self, phase):
        for copy in self.copies(phase):
            copy.start()

    def wait(self, phase):
        for copy in self.copies(phase):
            copy.wait()

    def swap(self):
        self.swap_copy(0).start()

    def scatter_a(self):
        r, l, core = self.refs, self.layer, self.place.core
        self.swap_copy(0).wait()
        for group in range(3):
            r.a_own[l, group] = low(f32(r.part[l, core, group]) + f32(r.sib[l, group]))
        self.start(0)

    def scatter_b(self):
        r, l = self.refs, self.layer
        self.wait(0)
        for group, (a, b, c) in enumerate(ORDERS):
            total = f32(r.a_own[l, group, part_of(self.place.at[a], 192)])
            for step in range(3):
                total += f32(r.a_in[l, group, step])
            r.b_own[l, group] = low(total).reshape(4, 48, 128)
        self.start(1)

    def share_c(self):
        r, l = self.refs, self.layer
        self.wait(1)
        for group, (a, b, c) in enumerate(ORDERS):
            total = f32(r.b_own[l, group, self.place.at[b]])
            for step in range(3):
                total += f32(r.b_in[l, group, step])
            r.c_all[l, group, self.place.at[c]] = low(total)
        self.start(2)

    def gather_b(self):
        r, l = self.refs, self.layer
        self.wait(2)
        for group, (a, b, c) in enumerate(ORDERS):
            total = f32(r.c_all[l, group, 0])
            for index in (1, 2, 3):
                total += f32(r.c_all[l, group, index])
            r.b_res[l, group, self.place.at[b]] = low(total)
        self.start(3)

    def gather_a(self):
        r, l = self.refs, self.layer
        self.wait(3)
        self.start(4)
        for group, (a, b, c) in enumerate(ORDERS):
            r.out[l, group, self.place.at[a], :, :, self.lanes] = r.b_res[l, group]

    def swap_back(self):
        self.wait(4)
        self.swap_copy(1).start()

    def end(self):
        self.swap_copy(1).wait()


class PlaneSum(KernelSum):
    def __init__(self, place, layer, refs):
        super().__init__(place, layer, refs)
        self.steps = [self.swap, self.scatter, self.share_c, self.gather_b, self.swap_back, self.end]

    def pieces(self, group):
        a, b, _ = ORDERS[group]
        for step in range(1, 16):
            to = {a: self.place.other(a, step // 4), b: self.place.other(b, step % 4)}
            yield step - 1, to[a], to[b], self.place.device(**to)

    def plane_wait(self, phase):
        r = self.refs
        for group in range(3):
            whole = r.p_in.at[group]
            remote(whole, whole, (r.p_send.at[phase, group], r.p_recv.at[phase, group]), self.place.sibling()).wait()

    def scatter(self):
        r, l, core = self.refs, self.layer, self.place.core
        self.swap_copy(0).wait()
        for group in range(3):
            r.a_own[l, group] = low(f32(r.part[l, core, group]) + f32(r.sib[l, group]))
        for group in range(3):
            sems = r.p_send.at[0, group], r.p_recv.at[0, group]
            for slot, to_a, to_b, device in self.pieces(group):
                piece = r.a_own.at[l, group, part_of(to_a * 4 + to_b, 48)]
                remote(piece, r.p_in.at[group, slot], sems, device).start()

    def share_c(self):
        r, l = self.refs, self.layer
        self.plane_wait(0)
        for group, (a, b, c) in enumerate(ORDERS):
            total = f32(r.a_own[l, group, part_of(self.place.at[a] * 4 + self.place.at[b], 48)])
            for slot in range(15):
                total += f32(r.p_in[group, slot])
            r.c_all[l, group, self.place.at[c]] = low(total)
        self.start(2)

    def gather_b(self):
        r, l = self.refs, self.layer
        self.wait(2)
        for group, (a, b, c) in enumerate(ORDERS):
            total = f32(r.c_all[l, group, 0])
            for index in (1, 2, 3):
                total += f32(r.c_all[l, group, index])
            mine = r.out.at[l, group, self.place.at[a], self.place.at[b], :, self.lanes]
            r.b_res[l, group, 0] = low(total)
            sems = r.p_send.at[1, group], r.p_recv.at[1, group]
            for _, _, _, device in self.pieces(group):
                remote(r.b_res.at[l, group, 0], mine, sems, device).start()
            mine[...] = low(total)

    def swap_back(self):
        self.plane_wait(1)
        self.swap_copy(1).start()


class EmbedSum(KernelSum):
    def __init__(self, place, refs):
        self.place, self.refs = place, refs
        self.lanes = part_of(place.core, 128)
        self.steps = [self.swap, self.scatter, self.share, self.gather, self.swap_back, self.end]

    def swap_copy(self, back):
        r, core = self.refs, self.place.core
        sems = r.e_swap_send.at[back], r.e_swap_recv.at[back]
        if back:
            mine = r.e_out.at[:, :, self.lanes]
            return remote(mine, mine, sems, self.place.sibling())
        return remote(r.e_part.at[1 - core], r.e_sib, sems, self.place.sibling())

    def copies(self, phase):
        r, mine, result = self.refs, self.place.at["z"], []
        for step in (1, 2, 3):
            to = self.place.other("z", step)
            src, dst = (r.e_own.at[to], r.e_in.at[step - 1]) if phase == 0 else (r.e_res, r.e_out.at[mine, :, self.lanes])
            sems = r.e_send.at[phase, step - 1], r.e_recv.at[phase, step - 1]
            result.append(remote(src, dst, sems, self.place.device(z=to)))
        return result

    def scatter(self):
        r = self.refs
        self.swap_copy(0).wait()
        r.e_own[...] = low(f32(r.e_part[self.place.core]) + f32(r.e_sib[...]))
        self.start(0)

    def share(self):
        r = self.refs
        self.wait(0)
        total = f32(r.e_own[self.place.at["z"]])
        for step in range(3):
            total += f32(r.e_in[step])
        r.e_plane[self.place.col] = low(total)
        mine = r.e_plane.at[self.place.col]
        for step in range(1, 16):
            device = (self.place.row, lax.rem(self.place.col + step, 16))
            remote(mine, mine, (r.e_plane_send, r.e_plane_recv), device).start()

    def gather(self):
        r = self.refs
        others = r.e_plane.at[0:15]
        remote(others, others, (r.e_plane_send, r.e_plane_recv), self.place.sibling()).wait()
        total = f32(r.e_plane[0])
        for index in range(1, 16):
            total += f32(r.e_plane[index])
        r.e_res[...] = low(total)
        self.start(1)
        r.e_out[self.place.at["z"], :, self.lanes] = low(total)

    def swap_back(self):
        self.wait(1)
        self.swap_copy(1).start()


def sigmoid(x):
    return 0.5 * jnp.tanh(0.5 * x) + 0.5


def silu_slope(hidden):
    sig = sigmoid(hidden)
    return sig * (1.0 + hidden * (1.0 - sig))


SIDES = ((0, -1), (0, 1), (-1, -1), (-1, 1), (1, -1), (1, 1))


class Halo:
    def __init__(self, place, refs, which, ext):
        self.place, self.refs, self.which, self.ext = place, refs, which, ext

    def copies(self):
        r, ext, result = self.refs, self.ext, []
        up, down = ext.at[8:16, 0:32], ext.at[32:40, 0:32]
        pairs = [((-1, 0), up, ext.at[40:48, 0:32]), ((1, 0), down, ext.at[0:8, 0:32])]
        for number, side in enumerate(SIDES):
            rows = part_of(number * 1, 256) if number < 2 else pl.ds(512 + (number - 2) * 64, 64)
            pairs.append((side, r.strip_out.at[self.which, rows], r.strip_in.at[self.which, rows]))
        for number, (side, src, dst) in enumerate(pairs):
            sems = r.halo_send.at[self.which, number], r.halo_recv.at[self.which, number]
            result.append(remote(src, dst, sems, self.place.grid_neighbour(*side)))
        return result

    def rows_of(self, number):
        return slice(number * 256, number * 256 + 256) if number < 2 else slice(512 + (number - 2) * 64, 576 + (number - 2) * 64)

    def start(self):
        r, ext = self.refs, self.ext
        for number, (down, right) in enumerate(SIDES):
            rows = {0: slice(8, 40), -1: slice(8, 16), 1: slice(32, 40)}[down]
            half = f32(ext[rows, 0:16] if right < 0 else ext[rows, 16:32])
            strip = half[:, 0:8] if right < 0 else half[:, 8:16]
            r.strip_out[self.which, self.rows_of(number)] = low(strip.reshape(-1, 256))
        for copy in self.copies():
            copy.start()

    def end(self):
        r, ext = self.refs, self.ext
        for copy in self.copies():
            copy.wait()
        for down, rows in ((0, slice(8, 40)), (1, slice(0, 8)), (-1, slice(40, 48))):
            strips = []
            for right in (-1, 1):
                strip = f32(r.strip_in[self.which, self.rows_of(SIDES.index((down, right)))])
                strips.append(strip.reshape(-1, 8, 256))
            ext[rows, 32:48] = low(jnp.concatenate(strips, axis=1))


class Stations:
    def __init__(self, place, refs):
        self.place, self.refs = place, refs

    def route(self):
        r = self.refs
        lane = lax.broadcasted_iota(jnp.int32, (512, DEVICES), 1)
        target = jnp.broadcast_to(f32(r.target[...]), (128, 512)).T
        marks = jnp.where(target == f32(lane), 1.0, 0.0)
        position = lax.broadcasted_iota(jnp.int32, (1, 512), 1)
        cell = jnp.where(position < r.count[0], r.cell[...], -1)
        halves = lax.broadcasted_iota(jnp.int32, (128, 512), 0) < 64
        where = jnp.where(halves, cell >> 5, cell & 31)
        info = low(f32(jnp.where(cell >= 0, where + 1, 0)).T)
        earlier = lax.broadcasted_iota(jnp.int32, (512, 512), 0) > lax.broadcasted_iota(jnp.int32, (512, 512), 1)
        before = jnp.dot(low(jnp.where(earlier, 1.0, 0.0)), low(marks), preferred_element_type=F32)
        rank = jnp.sum(before * marks, axis=1, keepdims=True)
        slot = target[:, 0:1] * 8.0 + rank
        picks = low(jnp.where(slot == f32(lax.broadcasted_iota(jnp.int32, (512, 1024), 1)), 1.0, 0.0))
        across = (((0,), (0,)), ((), ()))
        rows = lax.dot_general(picks, r.obs[...], across, preferred_element_type=F32).reshape(DEVICES, 8, 128)
        cells = lax.dot_general(picks, info, across, preferred_element_type=F32).reshape(DEVICES, 8, 128)
        r.st_out[...] = low(jnp.concatenate([rows, cells], axis=1))

    def send(self):
        r, place = self.refs, self.place

        def one(step, carry):
            number, device = place.by_step(step)
            remote(r.st_out.at[number], r.st_in.at[place.index], (r.st_send, r.st_recv), device).start()
            return carry

        lax.fori_loop(1, DEVICES, one, 0)
        r.st_in[place.index] = r.st_out[place.index]

    def receive(self):
        r = self.refs
        all_in = r.st_in.at[pl.ds(0, DEVICES - 1)]
        remote(all_in, all_in, (r.st_send, r.st_recv), self.place.by_step(1)[1]).wait()
        blocks = f32(r.st_in[...])
        r.rows[...] = low(blocks[:, 0:8].reshape(1024, 128))
        info = blocks[:, 8:16].reshape(1024, 128)
        r.cell_col[...] = info[:, 0:1] * 32.0 + info[:, 64:65] - 33.0
        turned = info.T
        cell_row = turned[0:1, :] * 32.0 + turned[64:65, :] - 33.0
        embedded = low(jnp.dot(r.rows[...], r.embed[...], preferred_element_type=F32))
        for part in range(4):
            cells = f32(lax.broadcasted_iota(jnp.int32, (256, 1024), 0) + part * 256)
            picks = low(jnp.where(cells == cell_row, 1.0, 0.0))
            placed = jnp.dot(picks, embedded, preferred_element_type=F32).reshape(8, 32, 256)
            own = slice(part * 8, part * 8 + 8)
            r.hid[0, part * 8 + 8 : part * 8 + 16, 0:32] = low(f32(r.base[own]) + placed)

    def gradient(self, grad_low):
        r = self.refs
        for part in range(2):
            rows = slice(part * 512, part * 512 + 512)
            cells = f32(lax.broadcasted_iota(jnp.int32, (512, 1024), 1))
            picks = low(jnp.where(cells == r.cell_col[rows], 1.0, 0.0))
            picked = low(jnp.dot(picks, grad_low, preferred_element_type=F32))
            total = lax.dot_general(r.rows[rows], picked, (((0,), (0,)), ((), ())), preferred_element_type=F32)
            yield total


def greet():
    place, barrier = Place(), pltpu.get_barrier_semaphore()

    def one(step, carry):
        pl.semaphore_signal(barrier, inc=1, device_id=place.by_step(step)[1], device_id_type=MESH)
        return carry

    lax.fori_loop(1, DEVICES, one, 0)
    return lambda: pl.semaphore_wait(barrier, DEVICES - 1)


class Convs:
    def __init__(self, place, refs):
        self.place, self.refs = place, refs

    def inside(self, first, rows):
        row = lax.broadcasted_iota(jnp.int32, (rows, EXT, 256), 0) + (first - 8 + self.place.row * 32)
        col = lax.broadcasted_iota(jnp.int32, (rows, EXT, 256), 1)
        col = jnp.where(col < 40, col, col - EXT) + self.place.col * 32
        return (row >= 0) & (row < 256) & (col >= 0) & (col < 512)

    def spread(self, value_of, out, spacing, sign, rows):
        first, last, size = rows

        def one(step, carry):
            row = first + step * size
            value = jnp.where(self.inside(row, size), value_of(row, size), 0.0)
            out[1, pl.ds(row, size)] = low(value)
            out[1 - sign, pl.ds(row, size)] = low(jnp.roll(value, spacing, axis=1))
            out[1 + sign, pl.ds(row, size)] = low(jnp.roll(value, -spacing, axis=1))
            return carry

        lax.fori_loop(0, (last - first) // size, one, 0)

    def activate(self, layer, rows):
        hid = self.refs.hid.at[layer]

        def value(row, size):
            x = f32(hid[pl.ds(row, size)])
            return x * sigmoid(x)

        self.spread(value, self.refs.act.at[layer], 2**layer, 1, rows)

    def taps(self, source, weights, row, size, width, spacing, sign, turned):
        total = None
        for i in range(3):
            for j in range(3):
                cells = source[j, pl.ds(row + sign * (i - 1) * spacing, size), 0:width].reshape(size * width, 256)
                contract = (((1,), (1 if turned else 0,)), ((), ()))
                term = lax.dot_general(cells, weights[3 * i + j], contract, preferred_element_type=F32)
                total = term if total is None else total + term
        return total.reshape(size, width, 256)

    def forward(self, layer, rows, width=EXT):
        r, (first, last, size) = self.refs, rows

        def one(step, carry):
            row = first + step * size
            update = self.taps(r.act.at[layer], r.weights.at[layer], row, size, width, 2**layer, 1, False)
            result = low(f32(r.hid[layer, pl.ds(row, size), 0:width]) + update)
            if layer == 2:
                r.block_out[pl.ds(row - 8, size)] = result
            else:
                r.hid[layer + 1, pl.ds(row, size)] = result
            return carry

        lax.fori_loop(0, (last - first) // size, one, 0)

    def kernel(self, layer):
        r, spacing = self.refs, 2**layer
        grad = r.grad_low[1, 8:40, 0:32].reshape(1024, 256)

        def one(j, carry):
            for i in range(3):
                row = 8 + (i - 1) * spacing
                cells = r.act[layer, j, row : row + 32, 0:32].reshape(1024, 256)
                total = lax.dot_general(cells, grad, (((0,), (0,)), ((), ())), preferred_element_type=F32)
                for half in range(2):
                    r.part[layer, half, i, part_of(j, 256)] = low(total[:, half * 128 : half * 128 + 128])
            return carry

        lax.fori_loop(0, 3, one, 0)

    def back(self, layer, rows, width=EXT):
        r, (first, last, size) = self.refs, rows

        def one(step, carry):
            row = first + step * size
            update = self.taps(r.grad_low, r.weights.at[layer], row, size, width, 2**layer, -1, True)
            before = f32(r.cot[pl.ds(row, size)]) if layer == 2 else r.grad[pl.ds(row, size), 0:width]
            result = before + update * silu_slope(f32(r.hid[layer, pl.ds(row, size), 0:width]))
            if layer == 0:
                r.base_grad[pl.ds(row - 8, size)] = result
            else:
                r.grad[pl.ds(row, size)] = result
            return carry

        lax.fori_loop(0, (last - first) // size, one, 0)

    def spread_grad(self, layer, rows):
        r = self.refs

        def value(row, size):
            return f32(r.cot[pl.ds(row, size)]) if layer == 2 else r.grad[pl.ds(row, size)]

        self.spread(value, r.grad_low, 2**layer, -1, rows)


class Refs:
    def __init__(self, names, refs):
        self.__dict__.update(zip(names, refs))


def whole_kernel(names, *refs):
    r = Refs(names, refs)
    place = Place()
    finish_greeting = greet()
    fetches = {}
    for number, name in enumerate(FETCHED):
        fetches[name] = pltpu.make_async_copy(getattr(r, name + "_hbm"), getattr(r, name), r.fetch.at[number])
        fetches[name].start()

    def fetched(*names):
        for name in names:
            fetches[name].wait()

    stations, convs = Stations(place, r), Convs(place, r)
    fetched("obs", "target", "cell")
    stations.route()
    fetched("cotangent")
    r.cot[8:40, 0:32] = r.cotangent[...]
    halo_cot, halo_hid = Halo(place, r, 0, r.cot), Halo(place, r, 1, r.hid.at[0])
    finish_greeting()
    stations.send()
    fetched("base", "embed")
    stations.receive()
    halo_hid.start()
    halo_cot.start()
    fetched("weights")
    halo_hid.end()
    convs.activate(0, (0, 48, 4))
    convs.forward(0, (2, 46, 11))
    convs.activate(1, (2, 46, 4))
    convs.forward(1, (4, 44, 10))
    halo_cot.end()
    convs.spread_grad(2, (0, 48, 4))
    convs.activate(2, (4, 44, 4))
    convs.forward(2, (8, 40, 16), 32)

    sums = {layer: KernelSum(place, layer, r).steps for layer in (1, 2)}
    sums[0] = PlaneSum(place, 0, r).steps
    sums["e"] = EmbedSum(place, r).steps

    def step(*which):
        for name in which:
            sums[name].pop(0)()

    convs.kernel(2)
    step(2)
    convs.back(2, (4, 44, 10))
    step(2)
    convs.spread_grad(1, (4, 44, 4))
    convs.kernel(1)
    step(1)
    convs.back(1, (6, 42, 9))
    step(2, 1)
    convs.spread_grad(0, (6, 42, 4))
    convs.kernel(0)
    step(0)
    convs.back(0, (8, 40, 16), 32)
    step(0, 2, 1)
    grad_low = low(r.base_grad[...].reshape(1024, 256))
    first, second = stations.gradient(grad_low)
    total = first + second
    for half in range(2):
        r.e_part[half] = low(total[:, half * 128 : half * 128 + 128]).reshape(4, 32, 128)
    step("e")
    while any(sums.values()):
        step(*[name for name in ("e", 0, 2, 1) if sums[name]])


SUM_SCRATCH = dict(
    part=pltpu.VMEM((3, 2, 3, 768, 128), BF),
    sib=pltpu.VMEM((3, 3, 768, 128), BF),
    a_own=pltpu.VMEM((3, 3, 768, 128), BF),
    a_in=pltpu.VMEM((3, 3, 3, 192, 128), BF),
    b_own=pltpu.VMEM((3, 3, 4, 48, 128), BF),
    b_in=pltpu.VMEM((3, 3, 3, 48, 128), BF),
    c_all=pltpu.VMEM((3, 3, 4, 48, 128), BF),
    b_res=pltpu.VMEM((3, 3, 4, 48, 128), BF),
    e_part=pltpu.VMEM((2, 4, 32, 128), BF),
    e_sib=pltpu.VMEM((4, 32, 128), BF),
    e_own=pltpu.VMEM((4, 32, 128), BF),
    e_in=pltpu.VMEM((3, 32, 128), BF),
    e_plane=pltpu.VMEM((16, 32, 128), BF),
    e_plane_send=pltpu.SemaphoreType.DMA,
    e_plane_recv=pltpu.SemaphoreType.DMA,
    p_in=pltpu.VMEM((3, 15, 48, 128), BF),
    p_send=pltpu.SemaphoreType.DMA((2, 3)),
    p_recv=pltpu.SemaphoreType.DMA((2, 3)),
    e_res=pltpu.VMEM((32, 128), BF),
    send=pltpu.SemaphoreType.DMA((3, 3, 5, 3)),
    recv=pltpu.SemaphoreType.DMA((3, 3, 5, 3)),
    swap_send=pltpu.SemaphoreType.DMA((3, 2)),
    swap_recv=pltpu.SemaphoreType.DMA((3, 2)),
    e_send=pltpu.SemaphoreType.DMA((2, 3)),
    e_recv=pltpu.SemaphoreType.DMA((2, 3)),
    e_swap_send=pltpu.SemaphoreType.DMA((2,)),
    e_swap_recv=pltpu.SemaphoreType.DMA((2,)),
)
SCRATCH = dict(
    SUM_SCRATCH,
    weights=pltpu.VMEM((3, 9, 256, 256), BF),
    base=pltpu.VMEM((32, 32, 256), BF),
    cotangent=pltpu.VMEM((32, 32, 256), BF),
    obs=pltpu.VMEM((512, 128), BF),
    embed=pltpu.VMEM((128, 256), BF),
    target=pltpu.VMEM((1, 512), jnp.int32),
    cell=pltpu.VMEM((1, 512), jnp.int32),
    fetch=pltpu.SemaphoreType.DMA((7,)),
    st_out=pltpu.VMEM((DEVICES, 16, 128), BF),
    st_in=pltpu.VMEM((DEVICES, 16, 128), BF),
    st_send=pltpu.SemaphoreType.DMA,
    st_recv=pltpu.SemaphoreType.DMA,
    rows=pltpu.VMEM((1024, 128), BF),
    cell_col=pltpu.VMEM((1024, 1), F32),
    cot=pltpu.VMEM((EXT, EXT, 256), BF),
    hid=pltpu.VMEM((3, EXT, EXT, 256), BF),
    act=pltpu.VMEM((3, 3, EXT, EXT, 256), BF),
    grad_low=pltpu.VMEM((3, EXT, EXT, 256), BF),
    grad=pltpu.VMEM((EXT, EXT, 256), F32),
    strip_out=pltpu.VMEM((2, 768, 256), BF),
    strip_in=pltpu.VMEM((2, 768, 256), BF),
    halo_send=pltpu.SemaphoreType.DMA((2, 8)),
    halo_recv=pltpu.SemaphoreType.DMA((2, 8)),
)
FETCHED = ("target", "cell", "obs", "base", "cotangent", "embed", "weights")
INPUTS = ("base_hbm", "obs_hbm", "target_hbm", "cell_hbm", "count", "embed_hbm", "weights_hbm", "cotangent_hbm")
OUTPUTS = ("block_out", "base_grad", "out", "e_out")


CHUNKS = 9


def finish_kernel(total, e_total, block, grad, conv_grads, embed_grad, block_out, base_grad, wide, e_wide, sems):
    scale = 1.0 / math.sqrt(131072)
    copies = [
        pltpu.make_async_copy(block, block_out, sems.at[CHUNKS]),
        pltpu.make_async_copy(grad, base_grad, sems.at[CHUNKS + 1]),
    ]
    for copy in copies:
        copy.start()
    for chunk in range(CHUNKS):
        wide[chunk] = f32(total[chunk]) * scale
        copies.append(pltpu.make_async_copy(wide.at[chunk], conv_grads.at[chunk], sems.at[chunk]))
        copies[-1].start()
    e_wide[...] = f32(e_total[...]) * scale
    copies.append(pltpu.make_async_copy(e_wide, embed_grad, sems.at[CHUNKS + 2]))
    copies[-1].start()
    for copy in copies:
        copy.wait()


def finish(total, e_total, block, grad):
    vmem, anywhere = pl.BlockSpec(memory_space=pltpu.VMEM), pl.BlockSpec(memory_space=pltpu.HBM)
    size = 6912 // CHUNKS
    return pl.pallas_call(
        finish_kernel,
        out_shape=[
            jax.ShapeDtypeStruct((CHUNKS, size, 256), F32),
            jax.ShapeDtypeStruct((128, 256), F32),
            jax.ShapeDtypeStruct((32, 32, 256), BF),
            jax.ShapeDtypeStruct((32, 32, 256), F32),
        ],
        in_specs=[vmem] * 4,
        out_specs=[anywhere] * 4,
        scratch_shapes=[
            pltpu.VMEM((CHUNKS, size, 256), F32),
            pltpu.VMEM((128, 256), F32),
            pltpu.SemaphoreType.DMA((CHUNKS + 3,)),
        ],
        compiler_params=pltpu.CompilerParams(vmem_limit_bytes=16 * 2**20),
        name="finish",
    )(total, e_total, block, grad)


def stay(array):
    return pltpu.with_memory_space_constraint(array, pltpu.HBM)


def local(
    base, observations, destination, cell_index, shard_counts, embed_weight, conv_weights, cotangent
):
    target, cell = destination.reshape(1, 512), cell_index.reshape(1, 512)
    vmem, hbm = pl.BlockSpec(memory_space=pltpu.VMEM), pl.BlockSpec(memory_space=pltpu.HBM)
    names = INPUTS + OUTPUTS + tuple(SCRATCH)
    block_out, base_grad, total, e_total = pl.pallas_call(
        lambda *refs: whole_kernel(names, *refs),
        out_shape=[
            jax.ShapeDtypeStruct((32, 32, 256), BF),
            jax.ShapeDtypeStruct((32, 32, 256), F32),
            jax.ShapeDtypeStruct((3, 3, 4, 4, 48, 256), BF),
            jax.ShapeDtypeStruct((4, 32, 256), BF),
        ],
        in_specs=[hbm, hbm, hbm, hbm, pl.BlockSpec(memory_space=pltpu.SMEM), hbm, hbm, hbm],
        out_specs=[vmem, vmem, vmem, vmem],
        scratch_shapes=list(SCRATCH.values()),
        compiler_params=pltpu.CompilerParams(
            collective_id=0, has_side_effects=True, vmem_limit_bytes=47 * 2**20
        ),
        name="station_block",
    )(
        stay(base), stay(observations), stay(target), stay(cell), shard_counts, stay(embed_weight),
        stay(conv_weights), stay(cotangent),
    )
    conv_grads, embed_grad, block_out, base_grad = finish(
        total.reshape(CHUNKS, 6912 // CHUNKS, 256), e_total.reshape(128, 256), block_out, base_grad
    )
    return (block_out, base_grad, conv_grads.reshape(3, 9, 256, 256), embed_grad)


def solution(mesh):
    return jax.shard_map(
        local,
        mesh=mesh,
        in_specs=(
            P("row", "col", None),
            P(("row", "col"), None),
            P(("row", "col"), None),
            P(("row", "col")),
            P(("row", "col")),
            P(),
            P(),
            P("row", "col", None),
        ),
        out_specs=(P("row", "col", None), P("row", "col", None), P(), P()),
        check_vma=False,
    )
```

```python
import math

import jax
import jax.numpy as jnp
from jax import lax
from jax.experimental import pallas as pl
from jax.experimental.pallas import tpu as pltpu
from jax.sharding import PartitionSpec as P

MESH = pl.DeviceIdType.MESH
BF = jnp.bfloat16
F32 = jnp.float32
ORDERS = (("x", "y", "z"), ("y", "z", "x"), ("z", "x", "y"))
EXT = 48
DEVICES = 128


def f32(value):
    return value.astype(F32)


def low(value):
    return value.astype(BF)


class Place:
    def __init__(self):
        self.row, self.col = lax.axis_index("row"), lax.axis_index("col")
        self.index = self.row * 16 + self.col
        self.core = lax.rem(self.row, 2)
        self.at = {"z": lax.div(self.row, 2), "y": lax.div(self.col, 4), "x": lax.rem(self.col, 4)}

    def device(self, **changed):
        at = {**self.at, "core": self.core, **changed}
        return (at["z"] * 2 + at["core"], at["y"] * 4 + at["x"])

    def other(self, axis, step):
        return lax.rem(self.at[axis] + step, 4)

    def sibling(self):
        return self.device(core=1 - self.core)

    def grid_neighbour(self, down, right):
        return (lax.rem(self.row + 8 + down, 8), lax.rem(self.col + 16 + right, 16))

    def by_step(self, step):
        number = lax.rem(self.index + step, DEVICES)
        return number, (lax.div(number, 16), lax.rem(number, 16))


def remote(src, dst, sems, device):
    return pltpu.make_async_remote_copy(
        src_ref=src, dst_ref=dst, send_sem=sems[0], recv_sem=sems[1], device_id=device, device_id_type=MESH
    )


def part_of(index, size):
    return pl.ds(pl.multiple_of(index * size, size), size)


class KernelSum:
    def __init__(self, place, layer, refs):
        self.place, self.layer, self.refs = place, layer, refs
        self.lanes = part_of(place.core, 128)
        self.steps = [
            self.scatter_a, self.scatter_b, self.share_c, self.gather_b, self.gather_a,
            self.swap_back, self.end,
        ]

    def swap_copy(self, back, group):
        r, l, core = self.refs, self.layer, self.place.core
        sems = r.swap_send.at[l, back, group], r.swap_recv.at[l, back, group]
        if back:
            mine = r.out.at[l, group, :, :, :, self.lanes]
            return remote(mine, mine, sems, self.place.sibling())
        return remote(r.part.at[l, 1 - core, group], r.sib.at[l, group], sems, self.place.sibling())

    def copies(self, phase):
        r, l = self.refs, self.layer
        result = []
        for group, (a, b, c) in enumerate(ORDERS):
            axis = (a, b, c, b, a)[phase]
            mine = self.place.at[axis]
            for step in (1, 2, 3):
                to = self.place.other(axis, step)
                src, dst = [
                    lambda: (r.a_own.at[l, group, part_of(to, 192)], r.a_in.at[l, group, step - 1]),
                    lambda: (r.b_own.at[l, group, to], r.b_in.at[l, group, step - 1]),
                    lambda: (r.c_all.at[l, group, mine], r.c_all.at[l, group, mine]),
                    lambda: (r.b_res.at[l, group, mine], r.b_res.at[l, group, mine]),
                    lambda: (r.b_res.at[l, group], r.out.at[l, group, mine, :, :, self.lanes]),
                ][phase]()
                sems = r.send.at[l, group, phase, step - 1], r.recv.at[l, group, phase, step - 1]
                result.append(remote(src, dst, sems, self.place.device(**{axis: to})))
        return result

    def start(self, phase):
        for copy in self.copies(phase):
            copy.start()

    def wait(self, phase):
        for copy in self.copies(phase):
            copy.wait()

    def swap(self, group):
        self.swap_copy(0, group).start()

    def scatter_a(self):
        r, l, core = self.refs, self.layer, self.place.core
        for group in range(3):
            self.swap_copy(0, group).wait()
            r.a_own[l, group] = low(f32(r.part[l, core, group]) + f32(r.sib[l, group]))
        self.start(0)

    def scatter_b(self):
        r, l = self.refs, self.layer
        self.wait(0)
        for group, (a, b, c) in enumerate(ORDERS):
            total = f32(r.a_own[l, group, part_of(self.place.at[a], 192)])
            for step in range(3):
                total += f32(r.a_in[l, group, step])
            r.b_own[l, group] = low(total).reshape(4, 48, 128)
        self.start(1)

    def share_c(self):
        r, l = self.refs, self.layer
        self.wait(1)
        for group, (a, b, c) in enumerate(ORDERS):
            total = f32(r.b_own[l, group, self.place.at[b]])
            for step in range(3):
                total += f32(r.b_in[l, group, step])
            r.c_all[l, group, self.place.at[c]] = low(total)
        self.start(2)

    def gather_b(self):
        r, l = self.refs, self.layer
        self.wait(2)
        for group, (a, b, c) in enumerate(ORDERS):
            total = f32(r.c_all[l, group, 0])
            for index in (1, 2, 3):
                total += f32(r.c_all[l, group, index])
            r.b_res[l, group, self.place.at[b]] = low(total)
        self.start(3)

    def gather_a(self):
        r, l = self.refs, self.layer
        self.wait(3)
        self.start(4)
        for group, (a, b, c) in enumerate(ORDERS):
            r.out[l, group, self.place.at[a], :, :, self.lanes] = r.b_res[l, group]

    def swap_back(self):
        self.wait(4)
        for group in range(3):
            self.swap_copy(1, group).start()

    def end(self):
        for group in range(3):
            self.swap_copy(1, group).wait()


class PlaneSum(KernelSum):
    def __init__(self, place, layer, refs, slot):
        super().__init__(place, layer, refs)
        self.slot = slot
        self.steps = [self.scatter, self.share_c, self.gather_b, self.swap_back, self.end]

    def pieces(self, group):
        a, b, _ = ORDERS[group]
        for step in range(1, 16):
            to = {a: self.place.other(a, step // 4), b: self.place.other(b, step % 4)}
            yield step - 1, to[a], to[b], self.place.device(**to)

    def plane_wait(self, phase, group):
        r, whole = self.refs, self.refs.p_in.at[self.slot, group]
        sems = r.p_send.at[self.slot, phase, group], r.p_recv.at[self.slot, phase, group]
        remote(whole, whole, sems, self.place.sibling()).wait()

    def scatter(self):
        r, l, core = self.refs, self.layer, self.place.core
        for group in range(3):
            self.swap_copy(0, group).wait()
            r.a_own[l, group] = low(f32(r.part[l, core, group]) + f32(r.sib[l, group]))
            sems = r.p_send.at[self.slot, 0, group], r.p_recv.at[self.slot, 0, group]
            for slot, to_a, to_b, device in self.pieces(group):
                piece = r.a_own.at[l, group, part_of(to_a * 4 + to_b, 48)]
                remote(piece, r.p_in.at[self.slot, group, slot], sems, device).start()

    def share_c(self):
        r, l = self.refs, self.layer
        for group, (a, b, c) in enumerate(ORDERS):
            self.plane_wait(0, group)
            total = f32(r.a_own[l, group, part_of(self.place.at[a] * 4 + self.place.at[b], 48)])
            for slot in range(15):
                total += f32(r.p_in[self.slot, group, slot])
            r.c_all[l, group, self.place.at[c]] = low(total)
        self.start(2)

    def gather_b(self):
        r, l = self.refs, self.layer
        self.wait(2)
        for group, (a, b, c) in enumerate(ORDERS):
            total = f32(r.c_all[l, group, 0])
            for index in (1, 2, 3):
                total += f32(r.c_all[l, group, index])
            mine = r.out.at[l, group, self.place.at[a], self.place.at[b], :, self.lanes]
            r.b_res[l, group, 0] = low(total)
            sems = r.p_send.at[self.slot, 1, group], r.p_recv.at[self.slot, 1, group]
            for _, _, _, device in self.pieces(group):
                remote(r.b_res.at[l, group, 0], mine, sems, device).start()
            mine[...] = low(total)

    def swap_back(self):
        for group in range(3):
            self.plane_wait(1, group)
            self.swap_copy(1, group).start()


class EmbedSum(KernelSum):
    def __init__(self, place, refs):
        self.place, self.refs = place, refs
        self.lanes = part_of(place.core, 128)
        self.steps = [self.scatter, self.share, self.gather, self.swap_back, self.end]

    def swap_copy(self, back):
        r, core = self.refs, self.place.core
        sems = r.e_swap_send.at[back], r.e_swap_recv.at[back]
        if back:
            mine = r.e_out.at[:, :, self.lanes]
            return remote(mine, mine, sems, self.place.sibling())
        return remote(r.e_part.at[1 - core], r.e_sib, sems, self.place.sibling())

    def copies(self, phase):
        r, mine, result = self.refs, self.place.at["z"], []
        for step in (1, 2, 3):
            to = self.place.other("z", step)
            src, dst = (r.e_own.at[to], r.e_in.at[step - 1]) if phase == 0 else (r.e_res, r.e_out.at[mine, :, self.lanes])
            sems = r.e_send.at[phase, step - 1], r.e_recv.at[phase, step - 1]
            result.append(remote(src, dst, sems, self.place.device(z=to)))
        return result

    def swap(self):
        self.swap_copy(0).start()

    def end(self):
        self.swap_copy(1).wait()

    def scatter(self):
        r = self.refs
        self.swap_copy(0).wait()
        r.e_own[...] = low(f32(r.e_part[self.place.core]) + f32(r.e_sib[...]))
        self.start(0)

    def share(self):
        r = self.refs
        self.wait(0)
        total = f32(r.e_own[self.place.at["z"]])
        for step in range(3):
            total += f32(r.e_in[step])
        r.e_plane[self.place.col] = low(total)
        mine = r.e_plane.at[self.place.col]
        for step in range(1, 16):
            device = (self.place.row, lax.rem(self.place.col + step, 16))
            remote(mine, mine, (r.e_plane_send, r.e_plane_recv), device).start()

    def gather(self):
        r = self.refs
        others = r.e_plane.at[0:15]
        remote(others, others, (r.e_plane_send, r.e_plane_recv), self.place.sibling()).wait()
        total = f32(r.e_plane[0])
        for index in range(1, 16):
            total += f32(r.e_plane[index])
        r.e_res[...] = low(total)
        self.start(1)
        r.e_out[self.place.at["z"], :, self.lanes] = low(total)

    def swap_back(self):
        self.wait(1)
        self.swap_copy(1).start()


def sigmoid(x):
    return 0.5 * jnp.tanh(0.5 * x) + 0.5


def silu_slope(hidden):
    sig = sigmoid(hidden)
    return sig * (1.0 + hidden * (1.0 - sig))


SIDES = ((0, -1), (0, 1), (-1, -1), (-1, 1), (1, -1), (1, 1))


class Halo:
    def __init__(self, place, refs, which, ext):
        self.place, self.refs, self.which, self.ext = place, refs, which, ext

    def copies(self):
        r, ext, result = self.refs, self.ext, []
        up, down = ext.at[8:16, 0:32], ext.at[32:40, 0:32]
        pairs = [((-1, 0), up, ext.at[40:48, 0:32]), ((1, 0), down, ext.at[0:8, 0:32])]
        for number, side in enumerate(SIDES):
            rows = part_of(number * 1, 256) if number < 2 else pl.ds(512 + (number - 2) * 64, 64)
            pairs.append((side, r.strip_out.at[self.which, rows], r.strip_in.at[self.which, rows]))
        for number, (side, src, dst) in enumerate(pairs):
            sems = r.halo_send.at[self.which, number], r.halo_recv.at[self.which, number]
            result.append(remote(src, dst, sems, self.place.grid_neighbour(*side)))
        return result

    def rows_of(self, number):
        return slice(number * 256, number * 256 + 256) if number < 2 else slice(512 + (number - 2) * 64, 576 + (number - 2) * 64)

    def start(self):
        r, ext = self.refs, self.ext
        for number, (down, right) in enumerate(SIDES):
            rows = {0: slice(8, 40), -1: slice(8, 16), 1: slice(32, 40)}[down]
            half = f32(ext[rows, 0:16] if right < 0 else ext[rows, 16:32])
            strip = half[:, 0:8] if right < 0 else half[:, 8:16]
            r.strip_out[self.which, self.rows_of(number)] = low(strip.reshape(-1, 256))
        for copy in self.copies():
            copy.start()

    def end(self):
        r, ext = self.refs, self.ext
        for copy in self.copies():
            copy.wait()
        for down, rows in ((0, slice(8, 40)), (1, slice(0, 8)), (-1, slice(40, 48))):
            strips = []
            for right in (-1, 1):
                strip = f32(r.strip_in[self.which, self.rows_of(SIDES.index((down, right)))])
                strips.append(strip.reshape(-1, 8, 256))
            ext[rows, 32:48] = low(jnp.concatenate(strips, axis=1))


class Stations:
    def __init__(self, place, refs):
        self.place, self.refs = place, refs

    def route(self):
        r = self.refs
        lane = lax.broadcasted_iota(jnp.int32, (512, DEVICES), 1)
        target = jnp.broadcast_to(f32(r.target[...]), (128, 512)).T
        marks = jnp.where(target == f32(lane), 1.0, 0.0)
        position = lax.broadcasted_iota(jnp.int32, (1, 512), 1)
        cell = jnp.where(position < r.count[0], r.cell[...], -1)
        halves = lax.broadcasted_iota(jnp.int32, (128, 512), 0) < 64
        where = jnp.where(halves, cell >> 5, cell & 31)
        info = low(f32(jnp.where(cell >= 0, where + 1, 0)).T)
        earlier = lax.broadcasted_iota(jnp.int32, (512, 512), 0) > lax.broadcasted_iota(jnp.int32, (512, 512), 1)
        before = jnp.dot(low(jnp.where(earlier, 1.0, 0.0)), low(marks), preferred_element_type=F32)
        rank = jnp.sum(before * marks, axis=1, keepdims=True)
        slot = target[:, 0:1] * 8.0 + rank
        picks = low(jnp.where(slot == f32(lax.broadcasted_iota(jnp.int32, (512, 1024), 1)), 1.0, 0.0))
        across = (((0,), (0,)), ((), ()))
        rows = lax.dot_general(picks, r.obs[...], across, preferred_element_type=F32).reshape(DEVICES, 8, 128)
        cells = lax.dot_general(picks, info, across, preferred_element_type=F32).reshape(DEVICES, 8, 128)
        r.st_out[...] = low(jnp.concatenate([rows, cells], axis=1))

    def send(self):
        r, place = self.refs, self.place

        def one(step, carry):
            number, device = place.by_step(step)
            remote(r.st_out.at[number], r.st_in.at[place.index], (r.st_send, r.st_recv), device).start()
            return carry

        lax.fori_loop(1, DEVICES, one, 0)
        r.st_in[place.index] = r.st_out[place.index]

    def receive(self):
        r = self.refs
        all_in = r.st_in.at[pl.ds(0, DEVICES - 1)]
        remote(all_in, all_in, (r.st_send, r.st_recv), self.place.by_step(1)[1]).wait()
        blocks = f32(r.st_in[...])
        r.rows[...] = low(blocks[:, 0:8].reshape(1024, 128))
        info = blocks[:, 8:16].reshape(1024, 128)
        r.cell_col[...] = info[:, 0:1] * 32.0 + info[:, 64:65] - 33.0
        turned = info.T
        cell_row = turned[0:1, :] * 32.0 + turned[64:65, :] - 33.0
        embedded = low(jnp.dot(r.rows[...], r.embed[...], preferred_element_type=F32))
        for part in range(4):
            cells = f32(lax.broadcasted_iota(jnp.int32, (256, 1024), 0) + part * 256)
            picks = low(jnp.where(cells == cell_row, 1.0, 0.0))
            placed = jnp.dot(picks, embedded, preferred_element_type=F32).reshape(8, 32, 256)
            own = slice(part * 8, part * 8 + 8)
            r.hid[0][part * 8 + 8 : part * 8 + 16, 0:32] = low(f32(r.base[own]) + placed)

    def embed_part(self):
        r = self.refs
        grad_low = low(r.base_grad[...].reshape(1024, 256))
        first, second = self.gradient(grad_low)
        total = first + second
        for half in range(2):
            r.e_part[half] = low(total[:, half * 128 : half * 128 + 128]).reshape(4, 32, 128)

    def gradient(self, grad_low):
        r = self.refs
        for part in range(2):
            rows = slice(part * 512, part * 512 + 512)
            cells = f32(lax.broadcasted_iota(jnp.int32, (512, 1024), 1))
            picks = low(jnp.where(cells == r.cell_col[rows], 1.0, 0.0))
            picked = low(jnp.dot(picks, grad_low, preferred_element_type=F32))
            total = lax.dot_general(r.rows[rows], picked, (((0,), (0,)), ((), ())), preferred_element_type=F32)
            yield total


def greet():
    place, barrier = Place(), pltpu.get_barrier_semaphore()

    def one(step, carry):
        pl.semaphore_signal(barrier, inc=1, device_id=place.by_step(step)[1], device_id_type=MESH)
        return carry

    lax.fori_loop(1, DEVICES, one, 0)
    return lambda: pl.semaphore_wait(barrier, DEVICES - 1)


class Convs:
    def __init__(self, place, refs):
        self.place, self.refs = place, refs

    def spread(self, value_of, out, spacing, sign):
        col = lax.broadcasted_iota(jnp.int32, (EXT, 256), 0)
        col = jnp.where(col < 40, col, col - EXT) + self.place.col * 32
        in_cols = f32((col >= 0) & (col < 512))

        def one(row, size):
            values = value_of(row, size)
            for k in range(size):
                grid_row = row + k - 8 + self.place.row * 32
                in_row = jnp.where((grid_row >= 0) & (grid_row < 256), 1.0, 0.0)
                value = jnp.where(in_cols * in_row > 0.0, values[k], 0.0)
                out[1, row + k] = low(value)
                out[1 - sign, row + k] = low(pltpu.roll(value, spacing, 0))
                out[1 + sign, row + k] = low(pltpu.roll(value, EXT - spacing, 0))

        return one

    def along(self, rows, work, behind=None):
        first, last, size = rows

        def one(step, carry):
            row = first + step * size
            if behind is not None:
                behind(row - size, size)
            work(row, size)
            return carry

        if behind is None:
            lax.fori_loop(0, (last - first) // size, one, 0)
        else:
            work(first, size)
            lax.fori_loop(1, (last - first) // size, one, 0)
            behind(last - size, size)

    def activation(self, layer):
        hid = self.refs.hid[layer]

        def value(row, size):
            x = f32(hid[pl.ds(row, size)])
            return x * sigmoid(x)

        return self.spread(value, self.refs.act[layer], 2**layer, 1)

    def taps(self, source, weights, row, size, width, spacing, sign, turned):
        total = None
        for i in range(3):
            for j in range(3):
                cells = source[j, pl.ds(row + sign * (i - 1) * spacing, size), 0:width].reshape(size * width, 256)
                contract = (((1,), (1 if turned else 0,)), ((), ()))
                term = lax.dot_general(cells, weights[3 * i + j], contract, preferred_element_type=F32)
                total = term if total is None else total + term
        return total.reshape(size, width, 256)

    def forward(self, layer, rows, width=EXT):
        r = self.refs

        def work(row, size):
            update = self.taps(r.act[layer], r.weights.at[layer], row, size, width, 2**layer, 1, False)
            result = low(f32(r.hid[layer][pl.ds(row, size), 0:width]) + update)
            if layer == 2:
                r.block_out[pl.ds(row - 8, size)] = result
            else:
                r.hid[layer + 1][pl.ds(row, size)] = result

        self.along(rows, work, None if layer == 2 else self.activation(layer + 1))

    def kernel(self, layer, then):
        r, spacing = self.refs, 2**layer
        grad = r.grad_low[layer % 2][1, 8:40, 0:32].reshape(1024, 256)
        for i in range(3):
            row = 8 + (i - 1) * spacing

            def one(j, carry):
                cells = r.act[layer][j, row : row + 32, 0:32].reshape(1024, 256)
                total = lax.dot_general(cells, grad, (((0,), (0,)), ((), ())), preferred_element_type=F32)
                for half in range(2):
                    r.part[layer, half, i, part_of(j, 256)] = low(total[:, half * 128 : half * 128 + 128])
                return carry

            lax.fori_loop(0, 3, one, 0)
            then(i)

    def back(self, layer, rows, width=EXT):
        r = self.refs

        def work(row, size):
            update = self.taps(r.grad_low[layer % 2], r.weights.at[layer], row, size, width, 2**layer, -1, True)
            before = f32(r.cot[pl.ds(row, size)]) if layer == 2 else r.grad[pl.ds(row, size), 0:width]
            result = before + update * silu_slope(f32(r.hid[layer][pl.ds(row, size), 0:width]))
            if layer == 0:
                r.base_grad[pl.ds(row - 8, size)] = result
            else:
                r.grad[pl.ds(row, size)] = result

        self.along(rows, work, self.gradient(layer - 1) if layer else None)

    def gradient(self, layer):
        r = self.refs

        def value(row, size):
            return f32(r.cot[pl.ds(row, size)]) if layer == 2 else r.grad[pl.ds(row, size)]

        return self.spread(value, r.grad_low[layer % 2], 2**layer, -1)


class Refs:
    def __init__(self, names, refs):
        self.__dict__.update(zip(names, refs))


def whole_kernel(names, *refs):
    r = Refs(names, refs)
    place = Place()
    finish_greeting = greet()
    fetches = {}
    for number, name in enumerate(FETCHED):
        fetches[name] = pltpu.make_async_copy(getattr(r, name + "_hbm"), getattr(r, name), r.fetch.at[number])
        fetches[name].start()

    def fetched(*names):
        for name in names:
            fetches[name].wait()

    stations, convs = Stations(place, r), Convs(place, r)
    fetched("obs", "target", "cell")
    stations.route()
    fetched("cotangent")
    r.cot[8:40, 0:32] = r.cotangent[...]
    halo_cot, halo_hid = Halo(place, r, 0, r.cot), Halo(place, r, 1, r.hid[0])
    finish_greeting()
    stations.send()
    halo_cot.start()
    fetched("base", "embed")
    stations.receive()
    halo_hid.start()
    fetched("weights")
    halo_cot.end()
    convs.along((0, 48, 4), convs.gradient(2))
    halo_hid.end()
    convs.along((0, 48, 4), convs.activation(0))
    convs.forward(0, (2, 46, 11))
    convs.forward(1, (4, 44, 10))
    sums = [KernelSum(place, 0, r), KernelSum(place, 1, r), KernelSum(place, 2, r), EmbedSum(place, r)]

    def step(which):
        sums[which].steps.pop(0)()

    convs.kernel(2, sums[2].swap)
    convs.back(2, (4, 44, 10))
    step(2)
    convs.kernel(1, sums[1].swap)
    convs.back(1, (6, 42, 9))
    step(1)
    step(2)
    convs.kernel(0, sums[0].swap)
    convs.forward(2, (8, 40, 16), 32)
    step(0)
    step(2)
    step(1)
    convs.back(0, (8, 40, 16), 32)
    stations.embed_part()
    sums[3].swap()
    step(0)
    step(3)
    step(2)
    step(1)
    step(0)
    step(3)
    step(2)
    step(1)
    step(0)
    step(3)
    step(2)
    step(1)
    step(0)
    step(3)
    step(2)
    step(1)
    step(0)
    step(3)
    step(1)
    step(0)


PLANES = 1
SUM_SCRATCH = dict(
    part=pltpu.VMEM((3, 2, 3, 768, 128), BF),
    sib=pltpu.VMEM((3, 3, 768, 128), BF),
    a_own=pltpu.VMEM((3, 3, 768, 128), BF),
    a_in=pltpu.VMEM((3, 3, 3, 192, 128), BF),
    b_own=pltpu.VMEM((3, 3, 4, 48, 128), BF),
    b_in=pltpu.VMEM((3, 3, 3, 48, 128), BF),
    c_all=pltpu.VMEM((3, 3, 4, 48, 128), BF),
    b_res=pltpu.VMEM((3, 3, 4, 48, 128), BF),
    e_part=pltpu.VMEM((2, 4, 32, 128), BF),
    e_sib=pltpu.VMEM((4, 32, 128), BF),
    e_own=pltpu.VMEM((4, 32, 128), BF),
    e_in=pltpu.VMEM((3, 32, 128), BF),
    e_plane=pltpu.VMEM((16, 32, 128), BF),
    e_plane_send=pltpu.SemaphoreType.DMA,
    e_plane_recv=pltpu.SemaphoreType.DMA,
    p_in=pltpu.VMEM((PLANES, 3, 15, 48, 128), BF),
    p_send=pltpu.SemaphoreType.DMA((PLANES, 2, 3)),
    p_recv=pltpu.SemaphoreType.DMA((PLANES, 2, 3)),
    e_res=pltpu.VMEM((32, 128), BF),
    send=pltpu.SemaphoreType.DMA((3, 3, 5, 3)),
    recv=pltpu.SemaphoreType.DMA((3, 3, 5, 3)),
    swap_send=pltpu.SemaphoreType.DMA((3, 2, 3)),
    swap_recv=pltpu.SemaphoreType.DMA((3, 2, 3)),
    e_send=pltpu.SemaphoreType.DMA((2, 3)),
    e_recv=pltpu.SemaphoreType.DMA((2, 3)),
    e_swap_send=pltpu.SemaphoreType.DMA((2,)),
    e_swap_recv=pltpu.SemaphoreType.DMA((2,)),
)
SCRATCH = dict(
    SUM_SCRATCH,
    weights=pltpu.VMEM((3, 9, 256, 256), BF),
    base=pltpu.VMEM((32, 32, 256), BF),
    cotangent=pltpu.VMEM((32, 32, 256), BF),
    obs=pltpu.VMEM((512, 128), BF),
    embed=pltpu.VMEM((128, 256), BF),
    target=pltpu.VMEM((1, 512), jnp.int32),
    cell=pltpu.VMEM((1, 512), jnp.int32),
    fetch=pltpu.SemaphoreType.DMA((7,)),
    st_out=pltpu.VMEM((DEVICES, 16, 128), BF),
    st_in=pltpu.VMEM((DEVICES, 16, 128), BF),
    st_send=pltpu.SemaphoreType.DMA,
    st_recv=pltpu.SemaphoreType.DMA,
    rows=pltpu.VMEM((1024, 128), BF),
    cell_col=pltpu.VMEM((1024, 1), F32),
    cot=pltpu.VMEM((EXT, EXT, 256), BF),
    hid=[pltpu.VMEM((EXT, EXT, 256), BF)] * 3,
    act=[pltpu.VMEM((3, EXT, EXT, 256), BF)] * 3,
    grad_low=[pltpu.VMEM((3, EXT, EXT, 256), BF)] * 2,
    grad=pltpu.VMEM((EXT, EXT, 256), F32),
    strip_out=pltpu.VMEM((2, 768, 256), BF),
    strip_in=pltpu.VMEM((2, 768, 256), BF),
    halo_send=pltpu.SemaphoreType.DMA((2, 8)),
    halo_recv=pltpu.SemaphoreType.DMA((2, 8)),
)
FETCHED = ("target", "cell", "obs", "base", "cotangent", "embed", "weights")
INPUTS = ("base_hbm", "obs_hbm", "target_hbm", "cell_hbm", "count", "embed_hbm", "weights_hbm", "cotangent_hbm")
OUTPUTS = ("block_out", "base_grad", "out", "e_out")


CHUNKS = 9


def finish_kernel(total, e_total, block, grad, conv_grads, embed_grad, block_out, base_grad, wide, e_wide, sems):
    scale = 1.0 / math.sqrt(131072)
    copies = [
        pltpu.make_async_copy(block, block_out, sems.at[CHUNKS]),
        pltpu.make_async_copy(grad, base_grad, sems.at[CHUNKS + 1]),
    ]
    for copy in copies:
        copy.start()
    for chunk in range(CHUNKS):
        wide[chunk] = f32(total[chunk]) * scale
        copies.append(pltpu.make_async_copy(wide.at[chunk], conv_grads.at[chunk], sems.at[chunk]))
        copies[-1].start()
    e_wide[...] = f32(e_total[...]) * scale
    copies.append(pltpu.make_async_copy(e_wide, embed_grad, sems.at[CHUNKS + 2]))
    copies[-1].start()
    for copy in copies:
        copy.wait()


def finish(total, e_total, block, grad):
    vmem, anywhere = pl.BlockSpec(memory_space=pltpu.VMEM), pl.BlockSpec(memory_space=pltpu.HBM)
    size = 6912 // CHUNKS
    return pl.pallas_call(
        finish_kernel,
        out_shape=[
            jax.ShapeDtypeStruct((CHUNKS, size, 256), F32),
            jax.ShapeDtypeStruct((128, 256), F32),
            jax.ShapeDtypeStruct((32, 32, 256), BF),
            jax.ShapeDtypeStruct((32, 32, 256), F32),
        ],
        in_specs=[vmem] * 4,
        out_specs=[anywhere] * 4,
        scratch_shapes=[
            pltpu.VMEM((CHUNKS, size, 256), F32),
            pltpu.VMEM((128, 256), F32),
            pltpu.SemaphoreType.DMA((CHUNKS + 3,)),
        ],
        compiler_params=pltpu.CompilerParams(vmem_limit_bytes=16 * 2**20),
        name="finish",
    )(total, e_total, block, grad)


def stay(array):
    return pltpu.with_memory_space_constraint(array, pltpu.HBM)


def local(
    base, observations, destination, cell_index, shard_counts, embed_weight, conv_weights, cotangent
):
    target, cell = destination.reshape(1, 512), cell_index.reshape(1, 512)
    vmem, hbm = pl.BlockSpec(memory_space=pltpu.VMEM), pl.BlockSpec(memory_space=pltpu.HBM)
    names = INPUTS + OUTPUTS + tuple(SCRATCH)
    block_out, base_grad, total, e_total = pl.pallas_call(
        lambda *refs: whole_kernel(names, *refs),
        out_shape=[
            jax.ShapeDtypeStruct((32, 32, 256), BF),
            jax.ShapeDtypeStruct((32, 32, 256), F32),
            jax.ShapeDtypeStruct((3, 3, 4, 4, 48, 256), BF),
            jax.ShapeDtypeStruct((4, 32, 256), BF),
        ],
        in_specs=[hbm, hbm, hbm, hbm, pl.BlockSpec(memory_space=pltpu.SMEM), hbm, hbm, hbm],
        out_specs=[vmem, vmem, vmem, vmem],
        scratch_shapes=list(SCRATCH.values()),
        compiler_params=pltpu.CompilerParams(
            collective_id=0, has_side_effects=True, vmem_limit_bytes=47 * 2**20
        ),
        name="station_block",
    )(
        stay(base), stay(observations), stay(target), stay(cell), shard_counts, stay(embed_weight),
        stay(conv_weights), stay(cotangent),
    )
    conv_grads, embed_grad, block_out, base_grad = finish(
        total.reshape(CHUNKS, 6912 // CHUNKS, 256), e_total.reshape(128, 256), block_out, base_grad
    )
    return (block_out, base_grad, conv_grads.reshape(3, 9, 256, 256), embed_grad)


def solution(mesh):
    return jax.shard_map(
        local,
        mesh=mesh,
        in_specs=(
            P("row", "col", None),
            P(("row", "col"), None),
            P(("row", "col"), None),
            P(("row", "col")),
            P(("row", "col")),
            P(),
            P(),
            P("row", "col", None),
        ),
        out_specs=(P("row", "col", None), P("row", "col", None), P(), P()),
        check_vma=False,
    )
```

```python
import math

import jax
import jax.numpy as jnp
from jax import lax
from jax.experimental import pallas as pl
from jax.experimental.pallas import tpu as pltpu
from jax.sharding import PartitionSpec as P

MESH = pl.DeviceIdType.MESH
BF = jnp.bfloat16
F32 = jnp.float32
ORDERS = (("x", "y", "z"), ("y", "z", "x"), ("z", "x", "y"))
EXT = 48
DEVICES = 128


def f32(value):
    return value.astype(F32)


def low(value):
    return value.astype(BF)


class Place:
    def __init__(self):
        self.row, self.col = lax.axis_index("row"), lax.axis_index("col")
        self.index = self.row * 16 + self.col
        self.core = lax.rem(self.row, 2)
        self.at = {"z": lax.div(self.row, 2), "y": lax.div(self.col, 4), "x": lax.rem(self.col, 4)}

    def device(self, **changed):
        at = {**self.at, "core": self.core, **changed}
        return (at["z"] * 2 + at["core"], at["y"] * 4 + at["x"])

    def other(self, axis, step):
        return lax.rem(self.at[axis] + step, 4)

    def sibling(self):
        return self.device(core=1 - self.core)

    def grid_neighbour(self, down, right):
        return (lax.rem(self.row + 8 + down, 8), lax.rem(self.col + 16 + right, 16))

    def by_step(self, step):
        number = lax.rem(self.index + step, DEVICES)
        return number, (lax.div(number, 16), lax.rem(number, 16))


def remote(src, dst, sems, device):
    return pltpu.make_async_remote_copy(
        src_ref=src, dst_ref=dst, send_sem=sems[0], recv_sem=sems[1], device_id=device, device_id_type=MESH
    )


def part_of(index, size):
    return pl.ds(pl.multiple_of(index * size, size), size)


class KernelSum:
    def __init__(self, place, layer, refs):
        self.place, self.layer, self.refs = place, layer, refs
        self.lanes = part_of(place.core, 128)
        self.steps = [
            self.scatter_a, self.scatter_b, self.share_c, self.gather_b, self.gather_a,
            self.swap_back, self.end,
        ]

    def swap_copy(self, back, group):
        r, l, core = self.refs, self.layer, self.place.core
        sems = r.swap_send.at[l, back, group], r.swap_recv.at[l, back, group]
        if back:
            mine = r.out.at[l, group, :, :, :, self.lanes]
            return remote(mine, mine, sems, self.place.sibling())
        return remote(r.part.at[l, 1 - core, group], r.sib.at[l, group], sems, self.place.sibling())

    def copies(self, phase):
        r, l = self.refs, self.layer
        result = []
        for group, (a, b, c) in enumerate(ORDERS):
            axis = (a, b, c, b, a)[phase]
            mine = self.place.at[axis]
            for step in (1, 2, 3):
                to = self.place.other(axis, step)
                src, dst = [
                    lambda: (r.a_own.at[l, group, part_of(to, 192)], r.a_in.at[l, group, step - 1]),
                    lambda: (r.b_own.at[l, group, to], r.b_in.at[l, group, step - 1]),
                    lambda: (r.c_all.at[l, group, mine], r.c_all.at[l, group, mine]),
                    lambda: (r.b_res.at[l, group, mine], r.b_res.at[l, group, mine]),
                    lambda: (r.b_res.at[l, group], r.out.at[l, group, mine, :, :, self.lanes]),
                ][phase]()
                sems = r.send.at[l, group, phase, step - 1], r.recv.at[l, group, phase, step - 1]
                result.append(remote(src, dst, sems, self.place.device(**{axis: to})))
        return result

    def start(self, phase):
        for copy in self.copies(phase):
            copy.start()

    def wait(self, phase):
        for copy in self.copies(phase):
            copy.wait()

    def swap(self, group):
        self.swap_copy(0, group).start()

    def scatter_a(self):
        r, l, core = self.refs, self.layer, self.place.core
        for group in range(3):
            self.swap_copy(0, group).wait()
            r.a_own[l, group] = low(f32(r.part[l, core, group]) + f32(r.sib[l, group]))
        self.start(0)

    def scatter_b(self):
        r, l = self.refs, self.layer
        self.wait(0)
        for group, (a, b, c) in enumerate(ORDERS):
            total = f32(r.a_own[l, group, part_of(self.place.at[a], 192)])
            for step in range(3):
                total += f32(r.a_in[l, group, step])
            r.b_own[l, group] = low(total).reshape(4, 48, 128)
        self.start(1)

    def share_c(self):
        r, l = self.refs, self.layer
        self.wait(1)
        for group, (a, b, c) in enumerate(ORDERS):
            total = f32(r.b_own[l, group, self.place.at[b]])
            for step in range(3):
                total += f32(r.b_in[l, group, step])
            r.c_all[l, group, self.place.at[c]] = low(total)
        self.start(2)

    def gather_b(self):
        r, l = self.refs, self.layer
        self.wait(2)
        for group, (a, b, c) in enumerate(ORDERS):
            total = f32(r.c_all[l, group, 0])
            for index in (1, 2, 3):
                total += f32(r.c_all[l, group, index])
            r.b_res[l, group, self.place.at[b]] = low(total)
        self.start(3)

    def gather_a(self):
        r, l = self.refs, self.layer
        self.wait(3)
        self.start(4)
        for group, (a, b, c) in enumerate(ORDERS):
            r.out[l, group, self.place.at[a], :, :, self.lanes] = r.b_res[l, group]

    def swap_back(self):
        self.wait(4)
        for group in range(3):
            self.swap_copy(1, group).start()

    def end(self):
        for group in range(3):
            self.swap_copy(1, group).wait()


class PlaneSum(KernelSum):
    def __init__(self, place, layer, refs, slot):
        super().__init__(place, layer, refs)
        self.slot = slot
        self.steps = [self.scatter, self.share_c, self.gather_b, self.swap_back, self.end]

    def pieces(self, group):
        a, b, _ = ORDERS[group]
        for step in range(1, 16):
            to = {a: self.place.other(a, step // 4), b: self.place.other(b, step % 4)}
            yield step - 1, to[a], to[b], self.place.device(**to)

    def plane_wait(self, phase, group):
        r, whole = self.refs, self.refs.p_in.at[self.slot, group]
        sems = r.p_send.at[self.slot, phase, group], r.p_recv.at[self.slot, phase, group]
        remote(whole, whole, sems, self.place.sibling()).wait()

    def scatter(self):
        r, l, core = self.refs, self.layer, self.place.core
        for group in range(3):
            self.swap_copy(0, group).wait()
            r.a_own[l, group] = low(f32(r.part[l, core, group]) + f32(r.sib[l, group]))
            sems = r.p_send.at[self.slot, 0, group], r.p_recv.at[self.slot, 0, group]
            for slot, to_a, to_b, device in self.pieces(group):
                piece = r.a_own.at[l, group, part_of(to_a * 4 + to_b, 48)]
                remote(piece, r.p_in.at[self.slot, group, slot], sems, device).start()

    def share_c(self):
        r, l = self.refs, self.layer
        for group, (a, b, c) in enumerate(ORDERS):
            self.plane_wait(0, group)
            total = f32(r.a_own[l, group, part_of(self.place.at[a] * 4 + self.place.at[b], 48)])
            for slot in range(15):
                total += f32(r.p_in[self.slot, group, slot])
            r.c_all[l, group, self.place.at[c]] = low(total)
        self.start(2)

    def gather_b(self):
        r, l = self.refs, self.layer
        self.wait(2)
        for group, (a, b, c) in enumerate(ORDERS):
            total = f32(r.c_all[l, group, 0])
            for index in (1, 2, 3):
                total += f32(r.c_all[l, group, index])
            mine = r.out.at[l, group, self.place.at[a], self.place.at[b], :, self.lanes]
            r.b_res[l, group, 0] = low(total)
            sems = r.p_send.at[self.slot, 1, group], r.p_recv.at[self.slot, 1, group]
            for _, _, _, device in self.pieces(group):
                remote(r.b_res.at[l, group, 0], mine, sems, device).start()
            mine[...] = low(total)

    def swap_back(self):
        for group in range(3):
            self.plane_wait(1, group)
            self.swap_copy(1, group).start()


class EmbedSum(KernelSum):
    def __init__(self, place, refs):
        self.place, self.refs = place, refs
        self.lanes = part_of(place.core, 128)
        self.steps = [self.scatter, self.share, self.gather, self.swap_back, self.end]

    def swap_copy(self, back):
        r, core = self.refs, self.place.core
        sems = r.e_swap_send.at[back], r.e_swap_recv.at[back]
        if back:
            mine = r.e_out.at[:, :, self.lanes]
            return remote(mine, mine, sems, self.place.sibling())
        return remote(r.e_part.at[1 - core], r.e_sib, sems, self.place.sibling())

    def copies(self, phase):
        r, mine, result = self.refs, self.place.at["z"], []
        for step in (1, 2, 3):
            to = self.place.other("z", step)
            src, dst = (r.e_own.at[to], r.e_in.at[step - 1]) if phase == 0 else (r.e_res, r.e_out.at[mine, :, self.lanes])
            sems = r.e_send.at[phase, step - 1], r.e_recv.at[phase, step - 1]
            result.append(remote(src, dst, sems, self.place.device(z=to)))
        return result

    def swap(self):
        self.swap_copy(0).start()

    def end(self):
        self.swap_copy(1).wait()

    def scatter(self):
        r = self.refs
        self.swap_copy(0).wait()
        r.e_own[...] = low(f32(r.e_part[self.place.core]) + f32(r.e_sib[...]))
        self.start(0)

    def share(self):
        r = self.refs
        self.wait(0)
        total = f32(r.e_own[self.place.at["z"]])
        for step in range(3):
            total += f32(r.e_in[step])
        r.e_plane[self.place.col] = low(total)
        mine = r.e_plane.at[self.place.col]
        for step in range(1, 16):
            device = (self.place.row, lax.rem(self.place.col + step, 16))
            remote(mine, mine, (r.e_plane_send, r.e_plane_recv), device).start()

    def gather(self):
        r = self.refs
        others = r.e_plane.at[0:15]
        remote(others, others, (r.e_plane_send, r.e_plane_recv), self.place.sibling()).wait()
        total = f32(r.e_plane[0])
        for index in range(1, 16):
            total += f32(r.e_plane[index])
        r.e_res[...] = low(total)
        self.start(1)
        r.e_out[self.place.at["z"], :, self.lanes] = low(total)

    def swap_back(self):
        self.wait(1)
        self.swap_copy(1).start()


def sigmoid(x):
    return 0.5 * jnp.tanh(0.5 * x) + 0.5


def silu_slope(hidden):
    sig = sigmoid(hidden)
    return sig * (1.0 + hidden * (1.0 - sig))


SIDES = ((0, -1), (0, 1), (-1, -1), (-1, 1), (1, -1), (1, 1))


class Halo:
    def __init__(self, place, refs, which, ext):
        self.place, self.refs, self.which, self.ext = place, refs, which, ext

    def copies(self):
        r, ext, result = self.refs, self.ext, []
        up, down = ext.at[8:16, 0:32], ext.at[32:40, 0:32]
        pairs = [((-1, 0), up, ext.at[40:48, 0:32]), ((1, 0), down, ext.at[0:8, 0:32])]
        for number, side in enumerate(SIDES):
            rows = part_of(number * 1, 256) if number < 2 else pl.ds(512 + (number - 2) * 64, 64)
            pairs.append((side, r.strip_out.at[self.which, rows], r.strip_in.at[self.which, rows]))
        for number, (side, src, dst) in enumerate(pairs):
            sems = r.halo_send.at[self.which, number], r.halo_recv.at[self.which, number]
            result.append(remote(src, dst, sems, self.place.grid_neighbour(*side)))
        return result

    def rows_of(self, number):
        return slice(number * 256, number * 256 + 256) if number < 2 else slice(512 + (number - 2) * 64, 576 + (number - 2) * 64)

    def start(self):
        r, ext = self.refs, self.ext
        for number, (down, right) in enumerate(SIDES):
            rows = {0: slice(8, 40), -1: slice(8, 16), 1: slice(32, 40)}[down]
            half = f32(ext[rows, 0:16] if right < 0 else ext[rows, 16:32])
            strip = half[:, 0:8] if right < 0 else half[:, 8:16]
            r.strip_out[self.which, self.rows_of(number)] = low(strip.reshape(-1, 256))
        for copy in self.copies():
            copy.start()

    def end(self):
        r, ext = self.refs, self.ext
        for copy in self.copies():
            copy.wait()
        for down, rows in ((0, slice(8, 40)), (1, slice(0, 8)), (-1, slice(40, 48))):
            strips = []
            for right in (-1, 1):
                strip = f32(r.strip_in[self.which, self.rows_of(SIDES.index((down, right)))])
                strips.append(strip.reshape(-1, 8, 256))
            ext[rows, 32:48] = low(jnp.concatenate(strips, axis=1))


class Stations:
    def __init__(self, place, refs):
        self.place, self.refs = place, refs

    def route(self):
        r = self.refs
        lane = lax.broadcasted_iota(jnp.int32, (512, DEVICES), 1)
        target = jnp.broadcast_to(f32(r.target[...]), (128, 512)).T
        marks = jnp.where(target == f32(lane), 1.0, 0.0)
        position = lax.broadcasted_iota(jnp.int32, (1, 512), 1)
        cell = jnp.where(position < r.count[0], r.cell[...], -1)
        halves = lax.broadcasted_iota(jnp.int32, (128, 512), 0) < 64
        where = jnp.where(halves, cell >> 5, cell & 31)
        info = low(f32(jnp.where(cell >= 0, where + 1, 0)).T)
        earlier = lax.broadcasted_iota(jnp.int32, (512, 512), 0) > lax.broadcasted_iota(jnp.int32, (512, 512), 1)
        before = jnp.dot(low(jnp.where(earlier, 1.0, 0.0)), low(marks), preferred_element_type=F32)
        rank = jnp.sum(before * marks, axis=1, keepdims=True)
        slot = target[:, 0:1] * 8.0 + rank
        picks = low(jnp.where(slot == f32(lax.broadcasted_iota(jnp.int32, (512, 1024), 1)), 1.0, 0.0))
        across = (((0,), (0,)), ((), ()))
        rows = lax.dot_general(picks, r.obs[...], across, preferred_element_type=F32).reshape(DEVICES, 8, 128)
        cells = lax.dot_general(picks, info, across, preferred_element_type=F32).reshape(DEVICES, 8, 128)
        r.st_out[...] = low(jnp.concatenate([rows, cells], axis=1))

    def send(self):
        r, place = self.refs, self.place

        def one(step, carry):
            number, device = place.by_step(step)
            remote(r.st_out.at[number], r.st_in.at[place.index], (r.st_send, r.st_recv), device).start()
            return carry

        lax.fori_loop(1, DEVICES, one, 0)
        r.st_in[place.index] = r.st_out[place.index]

    def receive(self):
        r = self.refs
        all_in = r.st_in.at[pl.ds(0, DEVICES - 1)]
        remote(all_in, all_in, (r.st_send, r.st_recv), self.place.by_step(1)[1]).wait()
        blocks = f32(r.st_in[...])
        r.rows[...] = low(blocks[:, 0:8].reshape(1024, 128))
        info = blocks[:, 8:16].reshape(1024, 128)
        r.cell_col[...] = info[:, 0:1] * 32.0 + info[:, 64:65] - 33.0
        turned = info.T
        cell_row = turned[0:1, :] * 32.0 + turned[64:65, :] - 33.0
        embedded = low(jnp.dot(r.rows[...], r.embed[...], preferred_element_type=F32))
        for part in range(4):
            cells = f32(lax.broadcasted_iota(jnp.int32, (256, 1024), 0) + part * 256)
            picks = low(jnp.where(cells == cell_row, 1.0, 0.0))
            placed = jnp.dot(picks, embedded, preferred_element_type=F32).reshape(8, 32, 256)
            own = slice(part * 8, part * 8 + 8)
            r.hid[0][part * 8 + 8 : part * 8 + 16, 0:32] = low(f32(r.base[own]) + placed)

    def embed_part(self):
        r = self.refs
        grad_low = low(r.base_grad[...].reshape(1024, 256))
        first, second = self.gradient(grad_low)
        total = first + second
        for half in range(2):
            r.e_part[half] = low(total[:, half * 128 : half * 128 + 128]).reshape(4, 32, 128)

    def gradient(self, grad_low):
        r = self.refs
        for part in range(2):
            rows = slice(part * 512, part * 512 + 512)
            cells = f32(lax.broadcasted_iota(jnp.int32, (512, 1024), 1))
            picks = low(jnp.where(cells == r.cell_col[rows], 1.0, 0.0))
            picked = low(jnp.dot(picks, grad_low, preferred_element_type=F32))
            total = lax.dot_general(r.rows[rows], picked, (((0,), (0,)), ((), ())), preferred_element_type=F32)
            yield total


def greet():
    place, barrier = Place(), pltpu.get_barrier_semaphore()

    def one(step, carry):
        pl.semaphore_signal(barrier, inc=1, device_id=place.by_step(step)[1], device_id_type=MESH)
        return carry

    lax.fori_loop(1, DEVICES, one, 0)
    return lambda: pl.semaphore_wait(barrier, DEVICES - 1)


class Convs:
    def __init__(self, place, refs):
        self.place, self.refs = place, refs

    def spread(self, value_of, out, spacing, sign):
        col = lax.broadcasted_iota(jnp.int32, (EXT, 256), 0)
        col = jnp.where(col < 40, col, col - EXT) + self.place.col * 32
        in_cols = f32((col >= 0) & (col < 512))

        def one(row, size):
            values = value_of(row, size)
            for k in range(size):
                grid_row = row + k - 8 + self.place.row * 32
                in_row = jnp.where((grid_row >= 0) & (grid_row < 256), 1.0, 0.0)
                value = jnp.where(in_cols * in_row > 0.0, values[k], 0.0)
                out[1, row + k] = low(value)
                out[1 - sign, row + k] = low(pltpu.roll(value, spacing, 0))
                out[1 + sign, row + k] = low(pltpu.roll(value, EXT - spacing, 0))

        return one

    def along(self, rows, work, behind=None):
        first, last, size = rows

        def one(step, carry):
            row = first + step * size
            if behind is not None:
                behind(row - size, size)
            work(row, size)
            return carry

        if behind is None:
            lax.fori_loop(0, (last - first) // size, one, 0)
        else:
            work(first, size)
            lax.fori_loop(1, (last - first) // size, one, 0)
            behind(last - size, size)

    def activation(self, layer):
        hid = self.refs.hid[layer]

        def value(row, size):
            x = f32(hid[pl.ds(row, size)])
            return x * sigmoid(x)

        return self.spread(value, self.refs.act[layer], 2**layer, 1)

    def taps(self, source, weights, row, size, width, spacing, sign, turned):
        total = None
        for i in range(3):
            for j in range(3):
                cells = source[j, pl.ds(row + sign * (i - 1) * spacing, size), 0:width].reshape(size * width, 256)
                contract = (((1,), (1 if turned else 0,)), ((), ()))
                term = lax.dot_general(cells, weights[3 * i + j], contract, preferred_element_type=F32)
                total = term if total is None else total + term
        return total.reshape(size, width, 256)

    def forward(self, layer, rows, width=EXT):
        r = self.refs

        def work(row, size):
            update = self.taps(r.act[layer], r.weights.at[layer], row, size, width, 2**layer, 1, False)
            result = low(f32(r.hid[layer][pl.ds(row, size), 0:width]) + update)
            if layer == 2:
                r.block_out[pl.ds(row - 8, size)] = result
            else:
                r.hid[layer + 1][pl.ds(row, size)] = result

        self.along(rows, work, None if layer == 2 else self.activation(layer + 1))

    def kernel(self, layer, then):
        r, spacing = self.refs, 2**layer
        grad = r.grad_low[layer % 2][1, 8:40, 0:32].reshape(1024, 256)
        for i in range(3):
            row = 8 + (i - 1) * spacing

            def one(j, carry):
                cells = r.act[layer][j, row : row + 32, 0:32].reshape(1024, 256)
                total = lax.dot_general(cells, grad, (((0,), (0,)), ((), ())), preferred_element_type=F32)
                for half in range(2):
                    r.part[layer, half, i, part_of(j, 256)] = low(total[:, half * 128 : half * 128 + 128])
                return carry

            lax.fori_loop(0, 3, one, 0)
            then(i)

    def back(self, layer, rows, width=EXT):
        r = self.refs

        def work(row, size):
            update = self.taps(r.grad_low[layer % 2], r.weights.at[layer], row, size, width, 2**layer, -1, True)
            before = f32(r.cot[pl.ds(row, size)]) if layer == 2 else r.grad[pl.ds(row, size), 0:width]
            result = before + update * silu_slope(f32(r.hid[layer][pl.ds(row, size), 0:width]))
            if layer == 0:
                r.base_grad[pl.ds(row - 8, size)] = result
            else:
                r.grad[pl.ds(row, size)] = result

        self.along(rows, work, self.gradient(layer - 1) if layer else None)

    def gradient(self, layer):
        r = self.refs

        def value(row, size):
            return f32(r.cot[pl.ds(row, size)]) if layer == 2 else r.grad[pl.ds(row, size)]

        return self.spread(value, r.grad_low[layer % 2], 2**layer, -1)


class Refs:
    def __init__(self, names, refs):
        self.__dict__.update(zip(names, refs))


def whole_kernel(names, *refs):
    r = Refs(names, refs)
    place = Place()
    finish_greeting = greet()
    fetches = {}
    for number, name in enumerate(FETCHED):
        fetches[name] = pltpu.make_async_copy(getattr(r, name + "_hbm"), getattr(r, name), r.fetch.at[number])
        fetches[name].start()

    def fetched(*names):
        for name in names:
            fetches[name].wait()

    stations, convs = Stations(place, r), Convs(place, r)
    fetched("obs", "target", "cell")
    stations.route()
    fetched("cotangent")
    r.cot[8:40, 0:32] = r.cotangent[...]
    halo_cot, halo_hid = Halo(place, r, 0, r.cot), Halo(place, r, 1, r.hid[0])
    finish_greeting()
    stations.send()
    halo_cot.start()
    fetched("base", "embed")
    stations.receive()
    halo_hid.start()
    fetched("weights")
    halo_cot.end()
    convs.along((0, 48, 4), convs.gradient(2))
    halo_hid.end()
    convs.along((0, 48, 4), convs.activation(0))
    convs.forward(0, (2, 46, 22))
    convs.forward(1, (4, 44, 20))
    sums = [KernelSum(place, 0, r), KernelSum(place, 1, r), KernelSum(place, 2, r), EmbedSum(place, r)]

    def step(which):
        sums[which].steps.pop(0)()

    convs.kernel(2, sums[2].swap)
    convs.back(2, (4, 44, 20))
    step(2)
    convs.kernel(1, sums[1].swap)
    convs.back(1, (6, 42, 18))
    step(1)
    step(2)
    convs.kernel(0, sums[0].swap)
    convs.forward(2, (8, 40, 16), 32)
    step(0)
    step(2)
    step(1)
    convs.back(0, (8, 40, 16), 32)
    stations.embed_part()
    sums[3].swap()
    step(0)
    step(3)
    step(2)
    step(1)
    step(0)
    step(3)
    step(2)
    step(1)
    step(0)
    step(3)
    step(2)
    step(1)
    step(0)
    step(3)
    step(2)
    step(1)
    step(0)
    step(3)
    step(1)
    step(0)


PLANES = 1
SUM_SCRATCH = dict(
    part=pltpu.VMEM((3, 2, 3, 768, 128), BF),
    sib=pltpu.VMEM((3, 3, 768, 128), BF),
    a_own=pltpu.VMEM((3, 3, 768, 128), BF),
    a_in=pltpu.VMEM((3, 3, 3, 192, 128), BF),
    b_own=pltpu.VMEM((3, 3, 4, 48, 128), BF),
    b_in=pltpu.VMEM((3, 3, 3, 48, 128), BF),
    c_all=pltpu.VMEM((3, 3, 4, 48, 128), BF),
    b_res=pltpu.VMEM((3, 3, 4, 48, 128), BF),
    e_part=pltpu.VMEM((2, 4, 32, 128), BF),
    e_sib=pltpu.VMEM((4, 32, 128), BF),
    e_own=pltpu.VMEM((4, 32, 128), BF),
    e_in=pltpu.VMEM((3, 32, 128), BF),
    e_plane=pltpu.VMEM((16, 32, 128), BF),
    e_plane_send=pltpu.SemaphoreType.DMA,
    e_plane_recv=pltpu.SemaphoreType.DMA,
    p_in=pltpu.VMEM((PLANES, 3, 15, 48, 128), BF),
    p_send=pltpu.SemaphoreType.DMA((PLANES, 2, 3)),
    p_recv=pltpu.SemaphoreType.DMA((PLANES, 2, 3)),
    e_res=pltpu.VMEM((32, 128), BF),
    send=pltpu.SemaphoreType.DMA((3, 3, 5, 3)),
    recv=pltpu.SemaphoreType.DMA((3, 3, 5, 3)),
    swap_send=pltpu.SemaphoreType.DMA((3, 2, 3)),
    swap_recv=pltpu.SemaphoreType.DMA((3, 2, 3)),
    e_send=pltpu.SemaphoreType.DMA((2, 3)),
    e_recv=pltpu.SemaphoreType.DMA((2, 3)),
    e_swap_send=pltpu.SemaphoreType.DMA((2,)),
    e_swap_recv=pltpu.SemaphoreType.DMA((2,)),
)
SCRATCH = dict(
    SUM_SCRATCH,
    weights=pltpu.VMEM((3, 9, 256, 256), BF),
    base=pltpu.VMEM((32, 32, 256), BF),
    cotangent=pltpu.VMEM((32, 32, 256), BF),
    obs=pltpu.VMEM((512, 128), BF),
    embed=pltpu.VMEM((128, 256), BF),
    target=pltpu.VMEM((1, 512), jnp.int32),
    cell=pltpu.VMEM((1, 512), jnp.int32),
    fetch=pltpu.SemaphoreType.DMA((7,)),
    st_out=pltpu.VMEM((DEVICES, 16, 128), BF),
    st_in=pltpu.VMEM((DEVICES, 16, 128), BF),
    st_send=pltpu.SemaphoreType.DMA,
    st_recv=pltpu.SemaphoreType.DMA,
    rows=pltpu.VMEM((1024, 128), BF),
    cell_col=pltpu.VMEM((1024, 1), F32),
    cot=pltpu.VMEM((EXT, EXT, 256), BF),
    hid=[pltpu.VMEM((EXT, EXT, 256), BF)] * 3,
    act=[pltpu.VMEM((3, EXT, EXT, 256), BF)] * 3,
    grad_low=[pltpu.VMEM((3, EXT, EXT, 256), BF)] * 2,
    grad=pltpu.VMEM((EXT, EXT, 256), F32),
    strip_out=pltpu.VMEM((2, 768, 256), BF),
    strip_in=pltpu.VMEM((2, 768, 256), BF),
    halo_send=pltpu.SemaphoreType.DMA((2, 8)),
    halo_recv=pltpu.SemaphoreType.DMA((2, 8)),
)
FETCHED = ("target", "cell", "obs", "base", "cotangent", "embed", "weights")
INPUTS = ("base_hbm", "obs_hbm", "target_hbm", "cell_hbm", "count", "embed_hbm", "weights_hbm", "cotangent_hbm")
OUTPUTS = ("block_out", "base_grad", "out", "e_out")


CHUNKS = 9


def finish_kernel(total, e_total, block, grad, conv_grads, embed_grad, block_out, base_grad, wide, e_wide, sems):
    scale = 1.0 / math.sqrt(131072)
    copies = [
        pltpu.make_async_copy(block, block_out, sems.at[CHUNKS]),
        pltpu.make_async_copy(grad, base_grad, sems.at[CHUNKS + 1]),
    ]
    for copy in copies:
        copy.start()
    for chunk in range(CHUNKS):
        wide[chunk] = f32(total[chunk]) * scale
        copies.append(pltpu.make_async_copy(wide.at[chunk], conv_grads.at[chunk], sems.at[chunk]))
        copies[-1].start()
    e_wide[...] = f32(e_total[...]) * scale
    copies.append(pltpu.make_async_copy(e_wide, embed_grad, sems.at[CHUNKS + 2]))
    copies[-1].start()
    for copy in copies:
        copy.wait()


def finish(total, e_total, block, grad):
    vmem, anywhere = pl.BlockSpec(memory_space=pltpu.VMEM), pl.BlockSpec(memory_space=pltpu.HBM)
    size = 6912 // CHUNKS
    return pl.pallas_call(
        finish_kernel,
        out_shape=[
            jax.ShapeDtypeStruct((CHUNKS, size, 256), F32),
            jax.ShapeDtypeStruct((128, 256), F32),
            jax.ShapeDtypeStruct((32, 32, 256), BF),
            jax.ShapeDtypeStruct((32, 32, 256), F32),
        ],
        in_specs=[vmem] * 4,
        out_specs=[anywhere] * 4,
        scratch_shapes=[
            pltpu.VMEM((CHUNKS, size, 256), F32),
            pltpu.VMEM((128, 256), F32),
            pltpu.SemaphoreType.DMA((CHUNKS + 3,)),
        ],
        compiler_params=pltpu.CompilerParams(vmem_limit_bytes=16 * 2**20),
        name="finish",
    )(total, e_total, block, grad)


def stay(array):
    return pltpu.with_memory_space_constraint(array, pltpu.HBM)


def local(
    base, observations, destination, cell_index, shard_counts, embed_weight, conv_weights, cotangent
):
    target, cell = destination.reshape(1, 512), cell_index.reshape(1, 512)
    vmem, hbm = pl.BlockSpec(memory_space=pltpu.VMEM), pl.BlockSpec(memory_space=pltpu.HBM)
    names = INPUTS + OUTPUTS + tuple(SCRATCH)
    block_out, base_grad, total, e_total = pl.pallas_call(
        lambda *refs: whole_kernel(names, *refs),
        out_shape=[
            jax.ShapeDtypeStruct((32, 32, 256), BF),
            jax.ShapeDtypeStruct((32, 32, 256), F32),
            jax.ShapeDtypeStruct((3, 3, 4, 4, 48, 256), BF),
            jax.ShapeDtypeStruct((4, 32, 256), BF),
        ],
        in_specs=[hbm, hbm, hbm, hbm, pl.BlockSpec(memory_space=pltpu.SMEM), hbm, hbm, hbm],
        out_specs=[vmem, vmem, vmem, vmem],
        scratch_shapes=list(SCRATCH.values()),
        compiler_params=pltpu.CompilerParams(
            collective_id=0, has_side_effects=True, vmem_limit_bytes=47 * 2**20
        ),
        name="station_block",
    )(
        stay(base), stay(observations), stay(target), stay(cell), shard_counts, stay(embed_weight),
        stay(conv_weights), stay(cotangent),
    )
    conv_grads, embed_grad, block_out, base_grad = finish(
        total.reshape(CHUNKS, 6912 // CHUNKS, 256), e_total.reshape(128, 256), block_out, base_grad
    )
    return (block_out, base_grad, conv_grads.reshape(3, 9, 256, 256), embed_grad)


def solution(mesh):
    return jax.shard_map(
        local,
        mesh=mesh,
        in_specs=(
            P("row", "col", None),
            P(("row", "col"), None),
            P(("row", "col"), None),
            P(("row", "col")),
            P(("row", "col")),
            P(),
            P(),
            P("row", "col", None),
        ),
        out_specs=(P("row", "col", None), P("row", "col", None), P(), P()),
        check_vma=False,
    )
```
